512 devices in a mesh: gx: 64 (over x, z), gy: 8 (over y, core).
Axes of the slice: x: 4, y: 4, z: 16, core: 2. Of those that a mesh axis runs over, the one named last changes fastest.
Arguments:
- background: float32 [64, 256, 64, 128], P(None, 'gx', 'gy'), may hold values from -1.0358009 to 1.0358009
- sensor_cells: int32 [64], replicated, may hold values from 0 to 2097151
- sensor_gain: float32 [64], replicated, may hold values from 1 to 4
- center: float32 [256, 64, 128], P('gx', 'gy'), may hold values from 0.4 to 0.9
- neighbours: float32 [6, 256, 64, 128], P(None, 'gx', 'gy'), may hold values from 0.02 to 0.16
Outputs:
- modes: float32 [64, 256, 64, 128], P(None, 'gx', 'gy')
- r_factor: float32 [64, 64], replicated
- first_r: float32 [64, 64], replicated
The draws below stay inside these ranges and needn't reach their ends.
All inputs are finite; a program needn't handle non-finite values.
Results may differ from the reference program's by a relative error of at most 0.0012.
Values sent between devices are 32-bit elements; how exact they have to be, the bound alone decides.
A program may use at most 64 MiB of HBM per device.

```python
import math
import jax
import jax.numpy as jnp
from jax import lax

K = 64
NZ = 128
NX = 256
NY = 64


def draw_background(key, part):
    root = math.sqrt(NX * NY * NZ)
    base = jax.random.fold_in(key, 11)
    key_shared, key_own, key_coef = jax.random.split(base, 3)
    coef = jax.random.uniform(key_coef, (K, 1, 1, 1), jnp.float32, 0.5, 1.5)
    place = jnp.arange(NX, dtype=jnp.float32).reshape(1, NX, 1, 1) / (NX - 1)
    ramp = 1.0 + 2.0 * place
    shared = jax.random.truncated_normal(key_shared, -4.0, 4.0, (1, NX, NY, NZ), jnp.float32)
    own = jax.random.truncated_normal(key_own, -4.0, 4.0, (K, NX, NY, NZ), jnp.float32)
    return 80.0 / root * coef * ramp * shared + 2.0 / root * own


def plant(drawn, key, low, top_value):
    shape = drawn.shape
    spot = [jax.random.randint(jax.random.fold_in(key, axis), (), 0, shape[axis]) for axis in range(len(shape))]
    drawn = drawn.at[tuple(spot)].set(low)
    longest = shape.index(max(shape))
    spot[longest] = (spot[longest] + 1) % shape[longest]
    return drawn.at[tuple(spot)].set(top_value)


def shard_levels(key, shape, cuts, least, largest):
    def one(axis_at, parts):
        draws = jax.random.uniform(jax.random.fold_in(jax.random.fold_in(key, 6), axis_at), (parts,), jnp.float32, least / len(cuts), largest / len(cuts))
        return jnp.repeat(jnp.exp(draws), shape[axis_at] // parts).reshape((-1,) + (1,) * (len(shape) - axis_at - 1))

    factor_of = one(*cuts[0])
    for cut in cuts[1:]:
        factor_of = factor_of * one(*cut)
    return factor_of


def setup_inputs(seed: int = 0) -> dict:
    streams_of = jax.random.split(jax.random.key(seed), 6)
    return {
        "background": draw_background(jax.random.fold_in(streams_of[5], 71), 0),
        "sensor_cells": plant(jax.random.randint(streams_of[1], (K,), 0, NX * NY * NZ), jax.random.fold_in(streams_of[1], 1), 0, (NX * NY * NZ) - 1).astype(jnp.int32),
        "sensor_gain": jnp.clip(jnp.exp(jax.random.uniform(streams_of[2], (K,), jnp.float32, math.log(1.0), math.log(4.0))), 1.0, 4.0),
        "center": jnp.clip(0.4 + 0.49999997 * jax.random.uniform(streams_of[3], (NX, NY, NZ), jnp.float32) ** shard_levels(streams_of[3], (NX, NY, NZ), ((0, 64), (1, 8)), -0.2, 0.2), 0.4, 0.9),
        "neighbours": jnp.clip(0.02 + 0.14 * jax.random.uniform(streams_of[4], (6, NX, NY, NZ), jnp.float32) ** shard_levels(streams_of[4], (6, NX, NY, NZ), ((1, 64), (2, 8)), -0.2, 0.2), 0.02, 0.16),
    }


def advance(padded, center, neighbours):
    core = padded[..., 1:-1, 1:-1, :]
    widths = [(0, 0)] * (core.ndim - 1) + [(1, 1)]
    zpadded = jnp.pad(core, widths)
    result = center * core
    result = result + neighbours[0] * padded[..., 2:, 1:-1, :]
    result = result + neighbours[1] * padded[..., :-2, 1:-1, :]
    result = result + neighbours[2] * padded[..., 1:-1, 2:, :]
    result = result + neighbours[3] * padded[..., 1:-1, :-2, :]
    result = result + neighbours[4] * zpadded[..., 2:]
    result = result + neighbours[5] * zpadded[..., :-2]
    return result

def reference(background, sensor_cells, sensor_gain, center, neighbours):
    count = background.shape[0]
    flat_state = background.reshape(count, -1)
    flat_state = flat_state.at[jnp.arange(count), sensor_cells].add(sensor_gain)
    adjoint = flat_state.reshape(background.shape)

    def twice(single):
        for repeat in range(2):
            padded = jnp.pad(single, ((1, 1), (1, 1), (0, 0)))
            single = advance(padded, center, neighbours)
        return single
    fields = lax.map(twice, adjoint)
    snapshot = fields.reshape(count, -1)
    gram_one = jnp.dot(snapshot, snapshot.T, precision=lax.Precision.HIGHEST)
    factor_one = jnp.linalg.cholesky(gram_one)
    basis_one = jax.scipy.linalg.solve_triangular(factor_one, snapshot, lower=True)
    gram_two = jnp.dot(basis_one, basis_one.T, precision=lax.Precision.HIGHEST)
    factor_two = jnp.linalg.cholesky(gram_two)
    basis_two = jax.scipy.linalg.solve_triangular(factor_two, basis_one, lower=True)
    upper = jnp.dot(factor_one, factor_two, precision=lax.Precision.HIGHEST).T
    root_cells = jnp.sqrt(jnp.float32(snapshot.shape[1]))
    modes = (basis_two * root_cells).reshape(background.shape)
    return (modes, upper / root_cells, factor_one.T / root_cells)
```

```python
import functools

import jax
import jax.numpy as jnp
from jax import lax
from jax.experimental import pallas as pl
from jax.experimental.pallas import tpu as pltpu
from jax.sharding import PartitionSpec as P

MESH = pl.DeviceIdType.MESH
F32 = jnp.float32
HIGHEST = lax.Precision.HIGHEST
ROW_CHUNKS = (0, 3, 1, 2)


def two_sum(a, b):
    s = a + b
    t = s - a
    return s, (a - (s - t)) + (b - t)


def power_below(m):
    q = m * F32(8388609.0)
    return jnp.abs(q - q * F32(0.99999994))


def pieces(s, big):
    first = (s + big) - big
    rest = s - first
    small = big * F32(1.0 / 256)
    second = (rest + small) - small
    return first, second, rest - second


def outer_sums(stacked):
    n = stacked.shape[0] // 3
    prod = lax.dot_general(stacked, stacked, (((1,), (1,)), ((), ())), preferred_element_type=F32)
    b = [[prod[i * n : (i + 1) * n, j * n : (j + 1) * n] for j in range(3)] for i in range(3)]
    mid, e1 = two_sum(b[0][1], b[1][0])
    high, e2 = two_sum(b[0][0], mid)
    low = ((b[0][2] + b[2][0]) + b[1][1]) + (b[1][2] + b[2][1]) + (e1 + e2)
    return high, low


class Group:
    def __init__(self, axis, digits):
        self.axis, self.digits = axis, digits
        self.size = 1
        for _, count in digits:
            self.size *= count

    def rank(self):
        me = lax.axis_index(self.axis)
        rank = 0
        for stride, count in self.digits:
            rank = rank * count + (me // stride) % count
        return rank

    def member(self, rank):
        me = lax.axis_index(self.axis)
        index = me
        for stride, count in reversed(self.digits):
            index = index + (rank % count - (me // stride) % count) * stride
            rank = rank // count
        return index


def groups_of(size_x):
    if size_x == 64:
        return [Group("gx", [(16, 4), (1, 2)]), Group("gx", [(2, 8)])]
    half = size_x // 2
    return [Group("gx", [(1, 2)]), Group("gx", [(2, half)])]


def sum_slots(buf, count, lanes):
    def body(i, carry):
        total, err = carry
        total, e = two_sum(total, buf[i])
        return total, err + e

    total, err = buf[0], jnp.zeros_like(buf[0])
    for i in range(1, count):
        total, err = body(i, (total, err))
    half = lanes // 2
    low = err + pltpu.roll(total, half, 1)
    high = total + low
    low = low - (high - total)
    lane = lax.broadcasted_iota(jnp.int32, high.shape, 1)
    return jnp.where(lane < half, high, pltpu.roll(low, half, 1))


def fields_kernel(
    nx, ny, cells_ref, gain_ref, bg_ref, cen_ref, nei_ref, s_out, g_out,
    bg_v, v_ref, w_ref, s_ref, rel_ref, gains_ref, xs_ref, pack_ref, piece_ref, buf0, buf1, buf2,
    load_sem, store_sem, x_send, x_recv, y_send, y_recv, r_send, r_recv,
):
    gx, gy = lax.axis_index("gx"), lax.axis_index("gy")
    width_x, width_y, k, lanes = 4, 8, v_ref.shape[2], v_ref.shape[3]
    y_group = Group("gy", [(1, ny)])
    groups = groups_of(nx)
    has_left, has_right = gx > 0, gx < nx - 1
    has_down, has_up = gy > 0, gy < ny - 1

    load = pltpu.make_async_copy(bg_ref, bg_v, load_sem)
    load.start()

    barrier = pltpu.get_barrier_semaphore()
    expected = 0
    for group in [y_group] + groups:
        rank = group.rank()
        for step in range(1, group.size):
            to = group.member((rank + step) % group.size)
            pl.semaphore_signal(barrier, inc=1, device_id={group.axis: to}, device_id_type=MESH)
            expected += 1

    @pl.when(has_left)
    def _():
        pl.semaphore_signal(barrier, inc=1, device_id={"gx": gx - 1}, device_id_type=MESH)

    @pl.when(has_right)
    def _():
        pl.semaphore_signal(barrier, inc=1, device_id={"gx": gx + 1}, device_id_type=MESH)

    zero_plane = jnp.zeros((width_y, k, lanes), F32)
    for edge, row in ((~has_left, 0), (~has_right, width_x + 1)):
        @pl.when(edge)
        def _(row=row):
            v_ref[row, 1 : width_y + 1] = zero_plane
            w_ref[row, 1 : width_y + 1] = zero_plane

    for edge, row in ((~has_down, 0), (~has_up, width_y + 1)):
        @pl.when(edge)
        def _(row=row):
            v_ref[1 : width_x + 1, row] = jnp.zeros((width_x, k, lanes), F32)
            w_ref[1 : width_x + 1, row] = jnp.zeros((width_x, k, lanes), F32)

    sub = lax.broadcasted_iota(jnp.int32, (k, lanes), 0)
    lane = lax.broadcasted_iota(jnp.int32, (k, lanes), 1)

    def spread(i, carry):
        cells, gains = carry
        here = sub == i
        return jnp.where(here, cells_ref[i], cells), jnp.where(here, gain_ref[i], gains)

    cells, gains = lax.fori_loop(0, k, spread, (jnp.zeros((k, lanes), jnp.int32), jnp.zeros((k, lanes), F32)))
    rel_ref[...] = cells - lane
    gains_ref[...] = gains

    load.wait()

    def take(i, _):
        x, y = i // width_y, i % width_y
        at = ((gx * width_x + x) * (width_y * ny) + gy * width_y + y) * lanes
        rows = bg_v[pl.ds(i, k, stride=width_x * width_y), :]
        v_ref[x + 1, y + 1] = rows + jnp.where(rel_ref[...] == at, gains_ref[...], 0.0)
        return 0

    lax.fori_loop(0, width_x * width_y, take, 0)
    pl.semaphore_wait(barrier, expected + has_left.astype(jnp.int32) + has_right.astype(jnp.int32))

    def x_copy(buf, which, c, side):
        rows = pl.ds(1 + 2 * c, 2)
        source, target = ((1, width_x + 1), (width_x, 0))[side]
        return pltpu.make_async_remote_copy(
            src_ref=buf.at[source, rows], dst_ref=buf.at[target, rows],
            send_sem=x_send.at[which, side, c], recv_sem=x_recv.at[which, side, c],
            device_id={"gx": (gx - 1, gx + 1)[side]}, device_id_type=MESH,
        )

    def y_copy(buf, which, side):
        source, target = ((1, width_y + 1), (width_y, 0))[side]
        planes = pl.ds(1, width_x)
        return pltpu.make_async_remote_copy(
            src_ref=buf.at[planes, source], dst_ref=buf.at[planes, target],
            send_sem=y_send.at[which, side], recv_sem=y_recv.at[which, side],
            device_id={"gy": (gy - 1, gy + 1)[side]}, device_id_type=MESH,
        )

    there_x, there_y = (has_left, has_right), (has_down, has_up)

    def start_x(buf, which, c):
        for side in (0, 1):
            @pl.when(there_x[side])
            def _(side=side):
                x_copy(buf, which, c, side).start()

    def start_y(buf, which, side):
        @pl.when(there_y[side])
        def _():
            y_copy(buf, which, side).start()

    def arrive_x(buf, which, c):
        for side in (0, 1):
            @pl.when(there_x[1 - side])
            def _(side=side):
                x_copy(buf, which, c, side).wait_recv()

    def arrive_y(buf, which, side):
        @pl.when(there_y[1 - side])
        def _():
            y_copy(buf, which, side).wait_recv()

    start_y(v_ref, 0, 0)
    start_y(v_ref, 0, 1)
    for c in ROW_CHUNKS:
        start_x(v_ref, 0, c)

    z_lane = lax.broadcasted_iota(jnp.int32, (1, lanes), 1)

    def advance(src, x, y):
        def row(ref):
            return jnp.broadcast_to(ref, (k, lanes))

        i = x * width_y + y
        core = src[x + 1, y + 1]
        upper = jnp.where(z_lane < lanes - 1, nei_ref[4, pl.ds(i, 1), :], 0.0)
        lower = jnp.where(z_lane > 0, nei_ref[5, pl.ds(i, 1), :], 0.0)
        result = row(cen_ref[pl.ds(i, 1), :]) * core
        result = result + row(nei_ref[0, pl.ds(i, 1), :]) * src[x + 2, y + 1]
        result = result + row(nei_ref[1, pl.ds(i, 1), :]) * src[x, y + 1]
        result = result + row(nei_ref[2, pl.ds(i, 1), :]) * src[x + 1, y + 2]
        result = result + row(nei_ref[3, pl.ds(i, 1), :]) * src[x + 1, y]
        result = result + row(upper) * pltpu.roll(core, lanes - 1, 1)
        result = result + row(lower) * pltpu.roll(core, 1, 1)
        return result

    arrive_y(v_ref, 0, 0)
    arrive_y(v_ref, 0, 1)
    for c in ROW_CHUNKS:
        arrive_x(v_ref, 0, c)

        def first(i, _, c=c):
            x, y = i // 2, 2 * c + i % 2
            w_ref[x + 1, y + 1] = advance(v_ref, x, y)
            return 0

        lax.fori_loop(0, 2 * width_x, first, 0)
        start_x(w_ref, 1, c)
        if c == 0:
            start_y(w_ref, 1, 0)
        if c == width_y // 2 - 1:
            start_y(w_ref, 1, 1)

    high = jnp.zeros((k, k), F32)
    low = jnp.zeros((k, k), F32)
    for turn, c in enumerate(ROW_CHUNKS):
        arrive_x(w_ref, 1, c)
        if c == 0:
            arrive_y(w_ref, 1, 1)
        if c == width_y // 2 - 1:
            arrive_y(w_ref, 1, 0)

        def second(i, most, c=c):
            x, y = i // 2, 2 * c + i % 2
            value = advance(w_ref, x, y)
            s_ref[c * 2 * width_x + i] = value
            return jnp.maximum(most, jnp.abs(value))

        most = lax.fori_loop(0, 2 * width_x, second, jnp.zeros((k, lanes), F32))
        part = pl.ds(c * 2 * width_x, 2 * width_x)
        pltpu.make_async_copy(s_ref.at[part], s_out.at[part], store_sem.at[c]).start()
        big = power_below(jnp.max(most, axis=1, keepdims=True)) * F32(1.5 * 2**17)
        for i in range(2 * width_x):
            for j, piece in enumerate(pieces(s_ref[c * 2 * width_x + i], big)):
                xs_ref[turn % 2, j * k : (j + 1) * k, i * lanes : (i + 1) * lanes] = piece.astype(jnp.bfloat16)
        part_high, part_low = outer_sums(xs_ref[turn % 2])
        high, e = two_sum(high, part_high)
        low = low + (part_low + e)

    pack_ref[...] = jnp.concatenate([high, low], axis=1)

    rows = k // ny
    y_rank = y_group.rank()

    def share(phase, group, source, target, slot, sem_slot):
        rank = group.rank()
        copies = []
        for step in range(1, group.size):
            peer = (rank + step) % group.size
            copies.append(pltpu.make_async_remote_copy(
                src_ref=source(peer), dst_ref=target(rank),
                send_sem=r_send.at[phase, step], recv_sem=r_recv.at[phase, rank],
                device_id={group.axis: group.member(peer)}, device_id_type=MESH,
            ))
        for copy in copies:
            copy.start()
        return copies

    def gather(phase, group, source, target):
        rank = group.rank()
        for step in range(1, group.size):
            peer = (rank + step) % group.size
            pltpu.make_async_remote_copy(
                src_ref=source(peer), dst_ref=target(peer),
                send_sem=r_send.at[phase, step], recv_sem=r_recv.at[phase, peer],
                device_id={group.axis: group.member(peer)}, device_id_type=MESH,
            ).wait_recv()

    sent = []

    def part_of(peer):
        return pack_ref.at[pl.ds(pl.multiple_of(peer * rows, rows), rows)]

    buf0[y_rank] = pack_ref[pl.ds(pl.multiple_of(y_rank * rows, rows), rows)]
    sent += share(0, y_group, part_of, lambda r: buf0.at[r], None, None)
    gather(0, y_group, part_of, lambda r: buf0.at[r])
    total = sum_slots(buf0, ny, lanes)
    for phase, (group, buf) in enumerate(zip(groups, (buf1, buf2)), 1):
        here = piece_ref.at[phase - 1]
        here[...] = total
        buf[group.rank()] = total
        sent += share(phase, group, lambda p: here, lambda r: buf.at[r], None, None)
        gather(phase, group, lambda p: here, lambda r: buf.at[r])
        total = sum_slots(buf, group.size, lanes)
    last = piece_ref.at[2]
    last[...] = total

    def rows_of(r):
        return g_out.at[pl.ds(pl.multiple_of(r * rows, rows), rows)]

    g_out[pl.ds(pl.multiple_of(y_rank * rows, rows), rows)] = total
    sent += share(3, y_group, lambda p: last, rows_of, None, None)
    gather(3, y_group, lambda p: last, rows_of)

    for copy in sent:
        copy.wait_send()
    for c in ROW_CHUNKS:
        part = pl.ds(c * 2 * width_x, 2 * width_x)
        pltpu.make_async_copy(s_ref.at[part], s_out.at[part], store_sem.at[c]).wait()
        for which, buf in enumerate((v_ref, w_ref)):
            for side in (0, 1):
                @pl.when(there_x[side])
                def _(c=c, which=which, buf=buf, side=side):
                    x_copy(buf, which, c, side).wait_send()
    for which, buf in enumerate((v_ref, w_ref)):
        for side in (0, 1):
            @pl.when(there_y[side])
            def _(which=which, buf=buf, side=side):
                y_copy(buf, which, side).wait_send()


def eliminate(a):
    n = a.shape[0]
    blocks = [a[8 * i : 8 * i + 8] for i in range(n // 8)]
    sub = lax.broadcasted_iota(jnp.int32, (8, 1), 0)
    for j in range(n):
        jb, jr = j // 8, j % 8
        row = blocks[jb][jr : jr + 1]
        scale = lax.rsqrt(row[:, j : j + 1])
        row = row * scale
        for i in range(jb, n // 8):
            update = (blocks[i][:, j : j + 1] * scale) * row
            if i == jb:
                blocks[i] = jnp.where(sub > jr, blocks[i] - update, jnp.where(sub == jr, row, blocks[i]))
            else:
                blocks[i] = blocks[i] - update
    return jnp.concatenate(blocks, axis=0)


def eye_mask(rows, columns):
    return lax.broadcasted_iota(jnp.int32, (rows, columns), 0) == lax.broadcasted_iota(jnp.int32, (rows, columns), 1)


def dot(a, b):
    return jnp.dot(a, b, precision=HIGHEST, preferred_element_type=F32)


def basis_kernel(root, s_hbm, g_ref, modes_ref, r_ref, first_ref, s_v, load_sem):
    k = g_ref.shape[0]
    load = pltpu.make_async_copy(s_hbm, s_v, load_sem)
    load.start()
    high, low = g_ref[:, :k], g_ref[:, k:]
    eye = eye_mask(k, k).astype(F32)
    row, column = lax.broadcasted_iota(jnp.int32, (k, k), 0), lax.broadcasted_iota(jnp.int32, (k, k), 1)
    upper = row <= column

    done = eliminate(jnp.concatenate([high, eye], axis=1))
    first = jnp.where(upper, done[:, :k], 0.0).T
    big = power_below(jnp.max(jnp.abs(first), axis=1, keepdims=True)) * F32(1.5 * 2**17)
    parts = [p.astype(jnp.bfloat16) for p in pieces(first, big)]
    first = (parts[2].astype(F32) + parts[1].astype(F32)) + parts[0].astype(F32)
    inverse = done[:, k:]
    full, rest = outer_sums(jnp.concatenate(parts, axis=0))
    left = (high - full) + (low - rest)
    gram = eye + dot(dot(inverse, left), inverse.T)

    done = eliminate(jnp.concatenate([gram, eye], axis=1))
    second_t = jnp.where(upper, done[:, :k], 0.0)
    weights = dot(done[:, k:], inverse) * root
    r_ref[...] = dot(second_t, first.T) * (1.0 / root)
    first_ref[...] = first.T * (1.0 / root)
    load.wait()
    count = s_v.shape[0]

    def body(i, _):
        x, y = i // 2 % (count // 8), i // (count // 4) * 2 + i % 2
        modes_ref[pl.ds(x * 8 + y, k, stride=count), :] = dot(weights, s_v[i])
        return 0

    lax.fori_loop(0, count, body, 0)


def local(nx, ny, background, sensor_cells, sensor_gain, center, neighbours):
    k, width_x, width_y, lanes = background.shape
    cells = width_x * width_y
    groups = groups_of(nx)
    vmem = pl.BlockSpec(memory_space=pltpu.VMEM)
    smem = pl.BlockSpec(memory_space=pltpu.SMEM)
    dma = pltpu.SemaphoreType.DMA
    slots = max([ny] + [g.size for g in groups])
    rows = k // ny
    fields, gram = pl.pallas_call(
        functools.partial(fields_kernel, nx, ny),
        out_shape=(jax.ShapeDtypeStruct((cells, k, lanes), F32), jax.ShapeDtypeStruct((k, 2 * k), F32)),
        in_specs=[smem, smem, pl.BlockSpec(memory_space=pl.ANY), vmem, vmem],
        out_specs=(pl.BlockSpec(memory_space=pl.ANY), vmem),
        scratch_shapes=[
            pltpu.VMEM((k * cells, lanes), F32),
            pltpu.VMEM((width_x + 2, width_y + 2, k, lanes), F32),
            pltpu.VMEM((width_x + 2, width_y + 2, k, lanes), F32),
            pltpu.VMEM((cells, k, lanes), F32),
            pltpu.VMEM((k, lanes), jnp.int32),
            pltpu.VMEM((k, lanes), F32),
            pltpu.VMEM((2, 3 * k, 2 * width_x * lanes), jnp.bfloat16),
            pltpu.VMEM((k, 2 * k), F32),
            pltpu.VMEM((3, rows, 2 * k), F32),
            pltpu.VMEM((ny, rows, 2 * k), F32),
            pltpu.VMEM((groups[0].size, rows, 2 * k), F32),
            pltpu.VMEM((groups[1].size, rows, 2 * k), F32),
            dma, dma((4,)),
            dma((2, 2, 4)), dma((2, 2, 4)), dma((2, 2)), dma((2, 2)),
            dma((4, slots)), dma((4, slots)),
        ],
        compiler_params=pltpu.CompilerParams(
            collective_id=0, has_side_effects=True, vmem_limit_bytes=24 * 2**20
        ),
        name="fields_and_products",
    )(
        sensor_cells, sensor_gain, background.reshape(k * cells, lanes),
        center.reshape(cells, lanes), neighbours.reshape(6, cells, lanes),
    )
    total_cells = cells * lanes * nx * ny
    root = float(total_cells) ** 0.5
    modes, r_factor, first_r = pl.pallas_call(
        functools.partial(basis_kernel, root),
        out_shape=(
            jax.ShapeDtypeStruct((k * cells, lanes), F32),
            jax.ShapeDtypeStruct((k, k), F32),
            jax.ShapeDtypeStruct((k, k), F32),
        ),
        in_specs=[pl.BlockSpec(memory_space=pl.ANY), vmem],
        out_specs=(vmem, vmem, vmem),
        scratch_shapes=[pltpu.VMEM((cells, k, lanes), F32), dma],
        compiler_params=pltpu.CompilerParams(vmem_limit_bytes=24 * 2**20),
        name="basis",
    )(fields, gram)
    return modes.reshape(background.shape), r_factor, first_r


def solution(mesh):
    nx, ny = mesh.shape["gx"], mesh.shape["gy"]
    in_specs = (P(None, "gx", "gy", None), P(), P(), P("gx", "gy", None), P(None, "gx", "gy", None))
    out_specs = (P(None, "gx", "gy", None), P(), P())
    return jax.shard_map(
        functools.partial(local, nx, ny), mesh=mesh, in_specs=in_specs, out_specs=out_specs, check_vma=False
    )
```

```python
import functools

import jax
import jax.numpy as jnp
from jax import lax
from jax.experimental import pallas as pl
from jax.experimental.pallas import tpu as pltpu
from jax.sharding import PartitionSpec as P

MESH = pl.DeviceIdType.MESH
F32 = jnp.float32
HIGHEST = lax.Precision.HIGHEST
ROW_CHUNKS = (0, 3, 1, 2)


def two_sum(a, b):
    s = a + b
    t = s - a
    return s, (a - (s - t)) + (b - t)


def power_below(m):
    q = m * F32(8388609.0)
    return jnp.abs(q - q * F32(0.99999994))


def pieces(s, big):
    first = (s + big) - big
    rest = s - first
    small = big * F32(1.0 / 256)
    second = (rest + small) - small
    return first, second, rest - second


def cut(a):
    big = power_below(jnp.max(jnp.abs(a), axis=1, keepdims=True)) * F32(1.5 * 2**17)
    return [p.astype(jnp.bfloat16) for p in pieces(a, big)]


def outer_sums(stacked):
    n = stacked.shape[0] // 3
    prod = lax.dot_general(stacked, stacked, (((1,), (1,)), ((), ())), preferred_element_type=F32)
    b = [[prod[i * n : (i + 1) * n, j * n : (j + 1) * n] for j in range(3)] for i in range(3)]
    mid, e1 = two_sum(b[0][1], b[1][0])
    high, e2 = two_sum(b[0][0], mid)
    low = ((b[0][2] + b[2][0]) + b[1][1]) + (b[1][2] + b[2][1]) + (e1 + e2)
    return high, low


class Group:
    def __init__(self, axis, digits):
        self.axis, self.digits = axis, digits
        self.size = 1
        for _, count in digits:
            self.size *= count

    def rank(self):
        me = lax.axis_index(self.axis)
        rank = 0
        for stride, count in self.digits:
            rank = rank * count + (me // stride) % count
        return rank

    def member(self, rank):
        me = lax.axis_index(self.axis)
        index = me
        for stride, count in reversed(self.digits):
            index = index + (rank % count - (me // stride) % count) * stride
            rank = rank // count
        return index


def groups_of(size_x):
    if size_x == 64:
        return [Group("gx", [(16, 4), (1, 2)]), Group("gx", [(2, 8)])]
    half = size_x // 2
    return [Group("gx", [(1, 2)]), Group("gx", [(2, half)])]


def sum_slots(buf, count, lanes):
    def body(i, carry):
        total, err = carry
        total, e = two_sum(total, buf[i])
        return total, err + e

    total, err = buf[0], jnp.zeros_like(buf[0])
    for i in range(1, count):
        total, err = body(i, (total, err))
    half = lanes // 2
    low = err + pltpu.roll(total, half, 1)
    high = total + low
    low = low - (high - total)
    lane = lax.broadcasted_iota(jnp.int32, high.shape, 1)
    return jnp.where(lane < half, high, pltpu.roll(low, half, 1))


def fields_kernel(
    nx, ny, cells_hbm, gain_hbm, bg_ref, cen_hbm, nei_hbm, xs_out, g_out,
    cells_ref, gain_ref, cen_ref, nei_ref, bg_v, v_ref, w_ref, s_ref, rel_ref, gains_ref, xs_ref, pack_ref, piece_ref, buf0, buf1, buf2,
    load_sem, store_sem, x_send, x_recv, y_send, y_recv, r_send, r_recv,
):
    gx, gy = lax.axis_index("gx"), lax.axis_index("gy")
    width_x, width_y, k, lanes = 4, 8, v_ref.shape[2], v_ref.shape[3]
    y_group = Group("gy", [(1, ny)])
    groups = groups_of(nx)
    has_left, has_right = gx > 0, gx < nx - 1
    has_down, has_up = gy > 0, gy < ny - 1

    loads = [
        pltpu.make_async_copy(source, target, load_sem.at[i])
        for i, (source, target) in enumerate((
            (bg_ref, bg_v), (cells_hbm, cells_ref), (gain_hbm, gain_ref), (cen_hbm, cen_ref), (nei_hbm, nei_ref),
        ))
    ]
    for load in loads:
        load.start()

    barrier = pltpu.get_barrier_semaphore()
    expected = 0
    for group in [y_group] + groups:
        rank = group.rank()
        for step in range(1, group.size):
            to = group.member((rank + step) % group.size)
            pl.semaphore_signal(barrier, inc=1, device_id={group.axis: to}, device_id_type=MESH)
            expected += 1

    @pl.when(has_left)
    def _():
        pl.semaphore_signal(barrier, inc=1, device_id={"gx": gx - 1}, device_id_type=MESH)

    @pl.when(has_right)
    def _():
        pl.semaphore_signal(barrier, inc=1, device_id={"gx": gx + 1}, device_id_type=MESH)

    zero_plane = jnp.zeros((width_y, k, lanes), F32)
    for edge, row in ((~has_left, 0), (~has_right, width_x + 1)):
        @pl.when(edge)
        def _(row=row):
            v_ref[row, 1 : width_y + 1] = zero_plane
            w_ref[row, 1 : width_y + 1] = zero_plane

    for edge, row in ((~has_down, 0), (~has_up, width_y + 1)):
        @pl.when(edge)
        def _(row=row):
            v_ref[1 : width_x + 1, row] = jnp.zeros((width_x, k, lanes), F32)
            w_ref[1 : width_x + 1, row] = jnp.zeros((width_x, k, lanes), F32)

    sub = lax.broadcasted_iota(jnp.int32, (k, lanes), 0)
    lane = lax.broadcasted_iota(jnp.int32, (k, lanes), 1)

    loads[1].wait()
    loads[2].wait()

    def spread(i, carry):
        cells, gains = carry
        here = sub == i
        return jnp.where(here, cells_ref[i], cells), jnp.where(here, gain_ref[i], gains)

    cells, gains = lax.fori_loop(
        0, k, spread, (jnp.zeros((k, lanes), jnp.int32), jnp.zeros((k, lanes), F32)), unroll=8
    )
    rel_ref[...] = cells - lane
    gains_ref[...] = gains

    loads[0].wait()

    def take(i, _):
        x, y = i // width_y, i % width_y
        at = ((gx * width_x + x) * (width_y * ny) + gy * width_y + y) * lanes
        rows = bg_v[pl.ds(i, k, stride=width_x * width_y), :]
        v_ref[x + 1, y + 1] = rows + jnp.where(rel_ref[...] == at, gains_ref[...], 0.0)
        return 0

    lax.fori_loop(0, width_x * width_y, take, 0, unroll=8)
    pl.semaphore_wait(barrier, expected + has_left.astype(jnp.int32) + has_right.astype(jnp.int32))

    def x_copy(buf, which, c, side):
        rows = pl.ds(1 + 2 * c, 2)
        source, target = ((1, width_x + 1), (width_x, 0))[side]
        return pltpu.make_async_remote_copy(
            src_ref=buf.at[source, rows], dst_ref=buf.at[target, rows],
            send_sem=x_send.at[which, side, c], recv_sem=x_recv.at[which, side, c],
            device_id={"gx": (gx - 1, gx + 1)[side]}, device_id_type=MESH,
        )

    def y_copy(buf, which, side):
        source, target = ((1, width_y + 1), (width_y, 0))[side]
        planes = pl.ds(1, width_x)
        return pltpu.make_async_remote_copy(
            src_ref=buf.at[planes, source], dst_ref=buf.at[planes, target],
            send_sem=y_send.at[which, side], recv_sem=y_recv.at[which, side],
            device_id={"gy": (gy - 1, gy + 1)[side]}, device_id_type=MESH,
        )

    there_x, there_y = (has_left, has_right), (has_down, has_up)

    def start_x(buf, which, c):
        for side in (0, 1):
            @pl.when(there_x[side])
            def _(side=side):
                x_copy(buf, which, c, side).start()

    def start_y(buf, which, side):
        @pl.when(there_y[side])
        def _():
            y_copy(buf, which, side).start()

    def arrive_x(buf, which, c):
        for side in (0, 1):
            @pl.when(there_x[1 - side])
            def _(side=side):
                x_copy(buf, which, c, side).wait_recv()

    def arrive_y(buf, which, side):
        @pl.when(there_y[1 - side])
        def _():
            y_copy(buf, which, side).wait_recv()

    start_y(v_ref, 0, 0)
    start_y(v_ref, 0, 1)
    for c in ROW_CHUNKS:
        start_x(v_ref, 0, c)

    z_lane = lax.broadcasted_iota(jnp.int32, (1, lanes), 1)

    def advance(src, x, y):
        def row(ref):
            return jnp.broadcast_to(ref, (k, lanes))

        i = x * width_y + y
        core = src[x + 1, y + 1]
        upper = jnp.where(z_lane < lanes - 1, nei_ref[4, pl.ds(i, 1), :], 0.0)
        lower = jnp.where(z_lane > 0, nei_ref[5, pl.ds(i, 1), :], 0.0)
        result = row(cen_ref[pl.ds(i, 1), :]) * core
        result = result + row(nei_ref[0, pl.ds(i, 1), :]) * src[x + 2, y + 1]
        result = result + row(nei_ref[1, pl.ds(i, 1), :]) * src[x, y + 1]
        result = result + row(nei_ref[2, pl.ds(i, 1), :]) * src[x + 1, y + 2]
        result = result + row(nei_ref[3, pl.ds(i, 1), :]) * src[x + 1, y]
        result = result + row(upper) * pltpu.roll(core, lanes - 1, 1)
        result = result + row(lower) * pltpu.roll(core, 1, 1)
        return result

    loads[3].wait()
    loads[4].wait()
    arrive_y(v_ref, 0, 0)
    arrive_y(v_ref, 0, 1)
    for c in ROW_CHUNKS:
        arrive_x(v_ref, 0, c)

        def first(i, _, c=c):
            x, y = i // 2, 2 * c + i % 2
            w_ref[x + 1, y + 1] = advance(v_ref, x, y)
            return 0

        lax.fori_loop(0, 2 * width_x, first, 0, unroll=True)
        start_x(w_ref, 1, c)
        if c == 0:
            start_y(w_ref, 1, 0)
        if c == width_y // 2 - 1:
            start_y(w_ref, 1, 1)

    high = jnp.zeros((k, k), F32)
    low = jnp.zeros((k, k), F32)
    for c in ROW_CHUNKS:
        arrive_x(w_ref, 1, c)
        if c == 0:
            arrive_y(w_ref, 1, 1)
        if c == width_y // 2 - 1:
            arrive_y(w_ref, 1, 0)

        def second(i, most, c=c):
            x, y = i // 2, 2 * c + i % 2
            value = advance(w_ref, x, y)
            s_ref[c * 2 * width_x + i] = value
            return jnp.maximum(most, jnp.abs(value))

        most = lax.fori_loop(0, 2 * width_x, second, jnp.zeros((k, lanes), F32), unroll=True)
        big = power_below(jnp.max(most, axis=1, keepdims=True)) * F32(1.5 * 2**17)
        for i in range(2 * width_x):
            for j, piece in enumerate(pieces(s_ref[c * 2 * width_x + i], big)):
                xs_ref[c, j * k : (j + 1) * k, i * lanes : (i + 1) * lanes] = piece.astype(jnp.bfloat16)
        pltpu.make_async_copy(xs_ref.at[c], xs_out.at[c], store_sem.at[c]).start()
        part_high, part_low = outer_sums(xs_ref[c])
        high, e = two_sum(high, part_high)
        low = low + (part_low + e)

    pack_ref[...] = jnp.concatenate([high, low], axis=1)

    rows = k // ny
    y_rank = y_group.rank()

    def share(phase, group, source, target, slot, sem_slot):
        rank = group.rank()
        copies = []
        for step in range(1, group.size):
            peer = (rank + step) % group.size
            copies.append(pltpu.make_async_remote_copy(
                src_ref=source(peer), dst_ref=target(rank),
                send_sem=r_send.at[phase, step], recv_sem=r_recv.at[phase, rank],
                device_id={group.axis: group.member(peer)}, device_id_type=MESH,
            ))
        for copy in copies:
            copy.start()
        return copies

    def gather(phase, group, source, target):
        rank = group.rank()
        for step in range(1, group.size):
            peer = (rank + step) % group.size
            pltpu.make_async_remote_copy(
                src_ref=source(peer), dst_ref=target(peer),
                send_sem=r_send.at[phase, step], recv_sem=r_recv.at[phase, peer],
                device_id={group.axis: group.member(peer)}, device_id_type=MESH,
            ).wait_recv()

    sent = []

    def part_of(peer):
        return pack_ref.at[pl.ds(pl.multiple_of(peer * rows, rows), rows)]

    buf0[y_rank] = pack_ref[pl.ds(pl.multiple_of(y_rank * rows, rows), rows)]
    sent += share(0, y_group, part_of, lambda r: buf0.at[r], None, None)
    gather(0, y_group, part_of, lambda r: buf0.at[r])
    total = sum_slots(buf0, ny, lanes)
    for phase, (group, buf) in enumerate(zip(groups, (buf1, buf2)), 1):
        here = piece_ref.at[phase - 1]
        here[...] = total
        buf[group.rank()] = total
        sent += share(phase, group, lambda p: here, lambda r: buf.at[r], None, None)
        gather(phase, group, lambda p: here, lambda r: buf.at[r])
        total = sum_slots(buf, group.size, lanes)
    last = piece_ref.at[2]
    last[...] = total

    def rows_of(r):
        return g_out.at[pl.ds(pl.multiple_of(r * rows, rows), rows)]

    g_out[pl.ds(pl.multiple_of(y_rank * rows, rows), rows)] = total
    sent += share(3, y_group, lambda p: last, rows_of, None, None)
    gather(3, y_group, lambda p: last, rows_of)

    for copy in sent:
        copy.wait_send()
    for c in ROW_CHUNKS:
        pltpu.make_async_copy(xs_ref.at[c], xs_out.at[c], store_sem.at[c]).wait()
        for which, buf in enumerate((v_ref, w_ref)):
            for side in (0, 1):
                @pl.when(there_x[side])
                def _(c=c, which=which, buf=buf, side=side):
                    x_copy(buf, which, c, side).wait_send()
    for which, buf in enumerate((v_ref, w_ref)):
        for side in (0, 1):
            @pl.when(there_y[side])
            def _(which=which, buf=buf, side=side):
                y_copy(buf, which, side).wait_send()


def eliminate(a):
    n, lanes = a.shape
    full = (8, lanes)
    blocks = [a[8 * i : 8 * i + 8] for i in range(n // 8)]
    sub = lax.broadcasted_iota(jnp.int32, full, 0)
    for p in range(n // 8):
        rest = range(p + 1, n // 8)
        own = blocks[p]

        def column(block, c, p=p):
            return jnp.broadcast_to(block[:, 8 * p + c : 8 * p + c + 1], full)

        rows = [jnp.broadcast_to(own[j : j + 1], full) for j in range(8)]
        own_columns = [column(own, c) for c in range(8)]
        d = {(i, c): jnp.broadcast_to(own_columns[c][i : i + 1], full) for c in range(8) for i in range(c + 1)}
        u = {i: [column(blocks[i], c) for c in range(8)] for i in rest}
        for j in range(8):
            scale = lax.rsqrt(d[j, j])
            rows[j] = rows[j] * scale
            factor = {c: d[j, c] * scale for c in range(j + 1, 8)}
            for c in range(j + 1, 8):
                for e in range(c, 8):
                    d[c, e] = d[c, e] - factor[c] * factor[e]
                rows[c] = rows[c] - factor[c] * rows[j]
            for i in rest:
                u[i][j] = u[i][j] * scale
                for c in range(j + 1, 8):
                    u[i][c] = u[i][c] - u[i][j] * factor[c]
                blocks[i] = blocks[i] - u[i][j] * rows[j]
        done = rows[0]
        for j in range(1, 8):
            done = jnp.where(sub == j, rows[j], done)
        blocks[p] = done
    return jnp.concatenate(blocks, axis=0)


def eye_mask(rows, columns):
    return lax.broadcasted_iota(jnp.int32, (rows, columns), 0) == lax.broadcasted_iota(jnp.int32, (rows, columns), 1)


def dot(a, b):
    return jnp.dot(a, b, precision=HIGHEST, preferred_element_type=F32)


def basis_kernel(root, xs_hbm, g_ref, modes_ref, r_ref, first_ref, xs_ref, out_ref, load_sem, store_sem):
    k = g_ref.shape[0]
    load = pltpu.make_async_copy(xs_hbm, xs_ref, load_sem)
    load.start()
    high, low = g_ref[:, :k], g_ref[:, k:]
    eye = eye_mask(k, k).astype(F32)
    row, column = lax.broadcasted_iota(jnp.int32, (k, k), 0), lax.broadcasted_iota(jnp.int32, (k, k), 1)
    upper = row <= column

    done = eliminate(jnp.concatenate([high, eye], axis=1))
    first = jnp.where(upper, done[:, :k], 0.0).T
    inverse = done[:, k:]
    parts = cut(first)
    first = (parts[2].astype(F32) + parts[1].astype(F32)) + parts[0].astype(F32)
    full, rest = outer_sums(jnp.concatenate(parts, axis=0))
    left = (high - full) + (low - rest)
    gram = eye + dot(dot(inverse, left), inverse.T)

    done = eliminate(jnp.concatenate([gram, eye], axis=1))
    second_t = jnp.where(upper, done[:, :k], 0.0)
    weights = jnp.concatenate([jnp.concatenate([p] * 3, axis=1) for p in cut(dot(done[:, k:], inverse) * root)], axis=0)
    load.wait()
    chunks, lanes = xs_ref.shape[0], out_ref.shape[-1]
    width_x = out_ref.shape[0]
    stores = []
    for x in range(width_x):
        for c in range(chunks):
            prod = jnp.dot(weights, xs_ref[c, :, 2 * lanes * x : 2 * lanes * (x + 1)], preferred_element_type=F32)
            prod = prod[:k] + (prod[k : 2 * k] + prod[2 * k :])
            for i in range(2):
                out_ref[x, :, 2 * c + i, :] = prod[:, i * lanes : (i + 1) * lanes]
        stores.append(pltpu.make_async_copy(out_ref.at[x], modes_ref.at[:, x], store_sem.at[x]))
        stores[-1].start()
    r_ref[...] = dot(second_t, first.T) * (1.0 / root)
    first_ref[...] = first.T * (1.0 / root)
    for store in stores:
        store.wait()


def local(nx, ny, background, sensor_cells, sensor_gain, center, neighbours):
    k, width_x, width_y, lanes = background.shape
    cells = width_x * width_y
    groups = groups_of(nx)
    vmem = pl.BlockSpec(memory_space=pltpu.VMEM)
    dma = pltpu.SemaphoreType.DMA
    slots = max([ny] + [g.size for g in groups])
    rows = k // ny
    pieces_shape = (width_y // 2, 3 * k, 2 * width_x * lanes)
    fields, gram = pl.pallas_call(
        functools.partial(fields_kernel, nx, ny),
        out_shape=(jax.ShapeDtypeStruct(pieces_shape, jnp.bfloat16), jax.ShapeDtypeStruct((k, 2 * k), F32)),
        in_specs=[pl.BlockSpec(memory_space=pltpu.HBM)] * 5,
        out_specs=(pl.BlockSpec(memory_space=pltpu.HBM), vmem),
        scratch_shapes=[
            pltpu.SMEM((k,), jnp.int32),
            pltpu.SMEM((k,), F32),
            pltpu.VMEM((cells, lanes), F32),
            pltpu.VMEM((6, cells, lanes), F32),
            pltpu.VMEM((k * cells, lanes), F32),
            pltpu.VMEM((width_x + 2, width_y + 2, k, lanes), F32),
            pltpu.VMEM((width_x + 2, width_y + 2, k, lanes), F32),
            pltpu.VMEM((cells, k, lanes), F32),
            pltpu.VMEM((k, lanes), jnp.int32),
            pltpu.VMEM((k, lanes), F32),
            pltpu.VMEM(pieces_shape, jnp.bfloat16),
            pltpu.VMEM((k, 2 * k), F32),
            pltpu.VMEM((3, rows, 2 * k), F32),
            pltpu.VMEM((ny, rows, 2 * k), F32),
            pltpu.VMEM((groups[0].size, rows, 2 * k), F32),
            pltpu.VMEM((groups[1].size, rows, 2 * k), F32),
            dma((5,)), dma((4,)),
            dma((2, 2, 4)), dma((2, 2, 4)), dma((2, 2)), dma((2, 2)),
            dma((4, slots)), dma((4, slots)),
        ],
        compiler_params=pltpu.CompilerParams(
            collective_id=0, has_side_effects=True, vmem_limit_bytes=56 * 2**20
        ),
        name="fields_and_products",
    )(
        sensor_cells, sensor_gain, background.reshape(k * cells, lanes),
        center.reshape(cells, lanes), neighbours.reshape(6, cells, lanes),
    )
    total_cells = cells * lanes * nx * ny
    root = float(total_cells) ** 0.5
    modes, r_factor, first_r = pl.pallas_call(
        functools.partial(basis_kernel, root),
        out_shape=(
            jax.ShapeDtypeStruct(background.shape, F32),
            jax.ShapeDtypeStruct((k, k), F32),
            jax.ShapeDtypeStruct((k, k), F32),
        ),
        in_specs=[pl.BlockSpec(memory_space=pltpu.HBM), vmem],
        out_specs=(pl.BlockSpec(memory_space=pltpu.HBM), vmem, vmem),
        scratch_shapes=[
            pltpu.VMEM(pieces_shape, jnp.bfloat16), pltpu.VMEM((width_x, k, width_y, lanes), F32), dma, dma((width_x,)),
        ],
        compiler_params=pltpu.CompilerParams(vmem_limit_bytes=56 * 2**20),
        name="basis",
    )(fields, gram)
    return modes, r_factor, first_r


def solution(mesh):
    nx, ny = mesh.shape["gx"], mesh.shape["gy"]
    in_specs = (P(None, "gx", "gy", None), P(), P(), P("gx", "gy", None), P(None, "gx", "gy", None))
    out_specs = (P(None, "gx", "gy", None), P(), P())
    return jax.shard_map(
        functools.partial(local, nx, ny), mesh=mesh, in_specs=in_specs, out_specs=out_specs, check_vma=False
    )
```

```python
import functools

import jax
import jax.numpy as jnp
from jax import lax
from jax.experimental import pallas as pl
from jax.experimental.pallas import tpu as pltpu
from jax.sharding import PartitionSpec as P

MESH = pl.DeviceIdType.MESH
F32 = jnp.float32
HIGHEST = lax.Precision.HIGHEST
ROW_CHUNKS = (0, 3, 1, 2)


def two_sum(a, b):
    s = a + b
    t = s - a
    return s, (a - (s - t)) + (b - t)


def power_below(m):
    q = m * F32(8388609.0)
    return jnp.abs(q - q * F32(0.99999994))


def pieces(s, big):
    first = (s + big) - big
    rest = s - first
    small = big * F32(1.0 / 256)
    second = (rest + small) - small
    return first, second, rest - second


def cut(a):
    big = power_below(jnp.max(jnp.abs(a), axis=1, keepdims=True)) * F32(1.5 * 2**17)
    return [p.astype(jnp.bfloat16) for p in pieces(a, big)]


def outer_sums(stacked):
    n = stacked.shape[0] // 3
    prod = lax.dot_general(stacked, stacked, (((1,), (1,)), ((), ())), preferred_element_type=F32)
    b = [[prod[i * n : (i + 1) * n, j * n : (j + 1) * n] for j in range(3)] for i in range(3)]
    mid, e1 = two_sum(b[0][1], b[1][0])
    high, e2 = two_sum(b[0][0], mid)
    low = ((b[0][2] + b[2][0]) + b[1][1]) + (b[1][2] + b[2][1]) + (e1 + e2)
    return high, low


class Group:
    def __init__(self, axis, digits):
        self.axis, self.digits = axis, digits
        self.size = 1
        for _, count in digits:
            self.size *= count

    def rank(self):
        me = lax.axis_index(self.axis)
        rank = 0
        for stride, count in self.digits:
            rank = rank * count + (me // stride) % count
        return rank

    def member(self, rank):
        me = lax.axis_index(self.axis)
        index = me
        for stride, count in reversed(self.digits):
            index = index + (rank % count - (me // stride) % count) * stride
            rank = rank // count
        return index


def groups_of(size_x):
    if size_x == 64:
        return [Group("gx", [(16, 4), (1, 2)]), Group("gx", [(2, 8)])]
    half = size_x // 2
    return [Group("gx", [(1, 2)]), Group("gx", [(2, half)])]


class Ring:
    def __init__(self, axis, stride, count):
        self.axis, self.stride, self.count = axis, stride, count

    def at(self, distance):
        me = lax.axis_index(self.axis)
        digit = (me // self.stride) % self.count
        steps = sorted({distance % self.count, -distance % self.count} - {0})
        return [{self.axis: me + ((digit + step) % self.count - digit) * self.stride} for step in steps]


def rings_of(nx, ny):
    deep = 16 if nx == 64 else nx
    return Ring("gx", 1, deep), Ring("gx", deep, nx // deep), Ring("gy", 2, ny // 2), Ring("gy", 1, 2)


def sum_slots(buf, count, lanes):
    def body(i, carry):
        total, err = carry
        total, e = two_sum(total, buf[i])
        return total, err + e

    total, err = buf[0], jnp.zeros_like(buf[0])
    for i in range(1, count):
        total, err = body(i, (total, err))
    half = lanes // 2
    low = err + pltpu.roll(total, half, 1)
    high = total + low
    low = low - (high - total)
    lane = lax.broadcasted_iota(jnp.int32, high.shape, 1)
    return jnp.where(lane < half, high, pltpu.roll(low, half, 1))


def fields_kernel(
    nx, ny, cells_hbm, gain_hbm, bg_ref, cen_hbm, nei_hbm, xs_out, g_out,
    cells_ref, gain_ref, cen_ref, nei_ref, bg_v, v_ref, w_ref, s_ref, rel_ref, gains_ref, xs_ref, pack_ref, piece_ref, buf0, buf1, buf2,
    news_sem, load_sem, store_sem, x_send, x_recv, y_send, y_recv, r_send, r_recv,
):
    gx, gy = lax.axis_index("gx"), lax.axis_index("gy")
    width_x, width_y, k, lanes = 4, 8, v_ref.shape[2], v_ref.shape[3]
    y_group = Group("gy", [(1, ny)])
    groups = groups_of(nx)
    has_left, has_right = gx > 0, gx < nx - 1
    has_down, has_up = gy > 0, gy < ny - 1

    loads = [
        pltpu.make_async_copy(source, target, load_sem.at[i])
        for i, (source, target) in enumerate((
            (bg_ref, bg_v), (cells_hbm, cells_ref), (gain_hbm, gain_ref), (cen_hbm, cen_ref), (nei_hbm, nei_ref),
        ))
    ]
    for load in loads:
        load.start()

    barrier = pltpu.get_barrier_semaphore()
    rings = rings_of(nx, ny)
    deep = rings[0]
    near = [to for ring in rings for to in ring.at(1)]
    rounds = (near, rings[3].at(1) + Ring("gx", 1, 2).at(1) + deep.at(2), deep.at(4))
    expected = len(near)

    def tell(sem, targets):
        for to in targets:
            pl.semaphore_signal(sem, inc=1, device_id=to, device_id_type=MESH)

    def hear(i):
        if rounds[i]:
            pl.semaphore_wait(news_sem.at[i], len(rounds[i]))

    tell(barrier, near)

    @pl.when(has_left)
    def _():
        pl.semaphore_signal(barrier, inc=1, device_id={"gx": gx - 1}, device_id_type=MESH)

    @pl.when(has_right)
    def _():
        pl.semaphore_signal(barrier, inc=1, device_id={"gx": gx + 1}, device_id_type=MESH)

    for there, to in ((has_down, gy - 1), (has_up, gy + 1)):
        @pl.when(there)
        def _(to=to):
            pl.semaphore_signal(barrier, inc=1, device_id={"gy": to}, device_id_type=MESH)

    zero_plane = jnp.zeros((width_y, k, lanes), F32)
    for edge, row in ((~has_left, 0), (~has_right, width_x + 1)):
        @pl.when(edge)
        def _(row=row):
            v_ref[row, 1 : width_y + 1] = zero_plane
            w_ref[row, 1 : width_y + 1] = zero_plane

    for edge, row in ((~has_down, 0), (~has_up, width_y + 1)):
        @pl.when(edge)
        def _(row=row):
            v_ref[1 : width_x + 1, row] = jnp.zeros((width_x, k, lanes), F32)
            w_ref[1 : width_x + 1, row] = jnp.zeros((width_x, k, lanes), F32)

    sub = lax.broadcasted_iota(jnp.int32, (k, lanes), 0)
    lane = lax.broadcasted_iota(jnp.int32, (k, lanes), 1)

    loads[1].wait()
    loads[2].wait()

    def spread(i, carry):
        cells, gains = carry
        here = sub == i
        return jnp.where(here, cells_ref[i], cells), jnp.where(here, gain_ref[i], gains)

    cells, gains = lax.fori_loop(
        0, k, spread, (jnp.zeros((k, lanes), jnp.int32), jnp.zeros((k, lanes), F32)), unroll=8
    )
    rel_ref[...] = cells - lane
    gains_ref[...] = gains

    loads[0].wait()

    def take(i, _):
        x, y = i // width_y, i % width_y
        at = ((gx * width_x + x) * (width_y * ny) + gy * width_y + y) * lanes
        rows = bg_v[pl.ds(i, k, stride=width_x * width_y), :]
        v_ref[x + 1, y + 1] = rows + jnp.where(rel_ref[...] == at, gains_ref[...], 0.0)
        return 0

    lax.fori_loop(0, width_x * width_y, take, 0, unroll=8)
    for there in (has_left, has_right, has_down, has_up):
        expected = expected + there.astype(jnp.int32)
    pl.semaphore_wait(barrier, expected)

    def x_copy(buf, which, c, side):
        rows = pl.ds(1 + 2 * c, 2)
        source, target = ((1, width_x + 1), (width_x, 0))[side]
        return pltpu.make_async_remote_copy(
            src_ref=buf.at[source, rows], dst_ref=buf.at[target, rows],
            send_sem=x_send.at[which, side, c], recv_sem=x_recv.at[which, side, c],
            device_id={"gx": (gx - 1, gx + 1)[side]}, device_id_type=MESH,
        )

    def y_copy(buf, which, side):
        source, target = ((1, width_y + 1), (width_y, 0))[side]
        planes = pl.ds(1, width_x)
        return pltpu.make_async_remote_copy(
            src_ref=buf.at[planes, source], dst_ref=buf.at[planes, target],
            send_sem=y_send.at[which, side], recv_sem=y_recv.at[which, side],
            device_id={"gy": (gy - 1, gy + 1)[side]}, device_id_type=MESH,
        )

    there_x, there_y = (has_left, has_right), (has_down, has_up)

    def start_x(buf, which, c):
        for side in (0, 1):
            @pl.when(there_x[side])
            def _(side=side):
                x_copy(buf, which, c, side).start()

    def start_y(buf, which, side):
        @pl.when(there_y[side])
        def _():
            y_copy(buf, which, side).start()

    def arrive_x(buf, which, c):
        for side in (0, 1):
            @pl.when(there_x[1 - side])
            def _(side=side):
                x_copy(buf, which, c, side).wait_recv()

    def arrive_y(buf, which, side):
        @pl.when(there_y[1 - side])
        def _():
            y_copy(buf, which, side).wait_recv()

    start_y(v_ref, 0, 0)
    start_y(v_ref, 0, 1)
    for c in ROW_CHUNKS:
        start_x(v_ref, 0, c)
    tell(news_sem.at[0], rounds[0])

    z_lane = lax.broadcasted_iota(jnp.int32, (1, lanes), 1)

    def advance(src, x, y):
        def row(ref):
            return jnp.broadcast_to(ref, (k, lanes))

        i = x * width_y + y
        core = src[x + 1, y + 1]
        upper = jnp.where(z_lane < lanes - 1, nei_ref[4, pl.ds(i, 1), :], 0.0)
        lower = jnp.where(z_lane > 0, nei_ref[5, pl.ds(i, 1), :], 0.0)
        result = row(cen_ref[pl.ds(i, 1), :]) * core
        result = result + row(nei_ref[0, pl.ds(i, 1), :]) * src[x + 2, y + 1]
        result = result + row(nei_ref[1, pl.ds(i, 1), :]) * src[x, y + 1]
        result = result + row(nei_ref[2, pl.ds(i, 1), :]) * src[x + 1, y + 2]
        result = result + row(nei_ref[3, pl.ds(i, 1), :]) * src[x + 1, y]
        result = result + row(upper) * pltpu.roll(core, lanes - 1, 1)
        result = result + row(lower) * pltpu.roll(core, 1, 1)
        return result

    loads[3].wait()
    loads[4].wait()
    arrive_y(v_ref, 0, 0)
    arrive_y(v_ref, 0, 1)
    for c in ROW_CHUNKS:
        arrive_x(v_ref, 0, c)

        def first(i, _, c=c):
            x, y = i // 2, 2 * c + i % 2
            w_ref[x + 1, y + 1] = advance(v_ref, x, y)
            return 0

        lax.fori_loop(0, 2 * width_x, first, 0, unroll=True)
        start_x(w_ref, 1, c)
        if c == 0:
            start_y(w_ref, 1, 0)
        if c == width_y // 2 - 1:
            start_y(w_ref, 1, 1)
        if c == ROW_CHUNKS[0]:
            hear(0)
            tell(news_sem.at[1], rounds[1])
        if c == ROW_CHUNKS[-1]:
            hear(1)
            tell(news_sem.at[2], rounds[2])

    high = jnp.zeros((k, k), F32)
    low = jnp.zeros((k, k), F32)
    for c in ROW_CHUNKS:
        arrive_x(w_ref, 1, c)
        if c == 0:
            arrive_y(w_ref, 1, 1)
        if c == width_y // 2 - 1:
            arrive_y(w_ref, 1, 0)

        def second(i, most, c=c):
            x, y = i // 2, 2 * c + i % 2
            value = advance(w_ref, x, y)
            s_ref[c * 2 * width_x + i] = value
            return jnp.maximum(most, jnp.abs(value))

        most = lax.fori_loop(0, 2 * width_x, second, jnp.zeros((k, lanes), F32), unroll=True)
        big = power_below(jnp.max(most, axis=1, keepdims=True)) * F32(1.5 * 2**17)
        for i in range(2 * width_x):
            for j, piece in enumerate(pieces(s_ref[c * 2 * width_x + i], big)):
                xs_ref[c, j * k : (j + 1) * k, i * lanes : (i + 1) * lanes] = piece.astype(jnp.bfloat16)
        pltpu.make_async_copy(xs_ref.at[c], xs_out.at[c], store_sem.at[c]).start()
        part_high, part_low = outer_sums(xs_ref[c])
        high, e = two_sum(high, part_high)
        low = low + (part_low + e)

    pack_ref[...] = jnp.concatenate([high, low], axis=1)

    rows = k // ny
    y_rank = y_group.rank()

    def share(phase, group, source, target, slot, sem_slot):
        rank = group.rank()
        copies = []
        for step in range(1, group.size):
            peer = (rank + step) % group.size
            copies.append(pltpu.make_async_remote_copy(
                src_ref=source(peer), dst_ref=target(rank),
                send_sem=r_send.at[phase, step], recv_sem=r_recv.at[phase, rank],
                device_id={group.axis: group.member(peer)}, device_id_type=MESH,
            ))
        for copy in copies:
            copy.start()
        return copies

    def gather(phase, group, source, target):
        rank = group.rank()
        for step in range(1, group.size):
            peer = (rank + step) % group.size
            pltpu.make_async_remote_copy(
                src_ref=source(peer), dst_ref=target(peer),
                send_sem=r_send.at[phase, step], recv_sem=r_recv.at[phase, peer],
                device_id={group.axis: group.member(peer)}, device_id_type=MESH,
            ).wait_recv()

    hear(2)
    sent = []

    def part_of(peer):
        return pack_ref.at[pl.ds(pl.multiple_of(peer * rows, rows), rows)]

    buf0[y_rank] = pack_ref[pl.ds(pl.multiple_of(y_rank * rows, rows), rows)]
    sent += share(0, y_group, part_of, lambda r: buf0.at[r], None, None)
    gather(0, y_group, part_of, lambda r: buf0.at[r])
    total = sum_slots(buf0, ny, lanes)
    for phase, (group, buf) in enumerate(zip(groups, (buf1, buf2)), 1):
        here = piece_ref.at[phase - 1]
        here[...] = total
        buf[group.rank()] = total
        sent += share(phase, group, lambda p: here, lambda r: buf.at[r], None, None)
        gather(phase, group, lambda p: here, lambda r: buf.at[r])
        total = sum_slots(buf, group.size, lanes)
    last = piece_ref.at[2]
    last[...] = total

    def rows_of(r):
        return g_out.at[pl.ds(pl.multiple_of(r * rows, rows), rows)]

    g_out[pl.ds(pl.multiple_of(y_rank * rows, rows), rows)] = total
    sent += share(3, y_group, lambda p: last, rows_of, None, None)
    gather(3, y_group, lambda p: last, rows_of)

    for copy in sent:
        copy.wait_send()
    for c in ROW_CHUNKS:
        pltpu.make_async_copy(xs_ref.at[c], xs_out.at[c], store_sem.at[c]).wait()
        for which, buf in enumerate((v_ref, w_ref)):
            for side in (0, 1):
                @pl.when(there_x[side])
                def _(c=c, which=which, buf=buf, side=side):
                    x_copy(buf, which, c, side).wait_send()
    for which, buf in enumerate((v_ref, w_ref)):
        for side in (0, 1):
            @pl.when(there_y[side])
            def _(which=which, buf=buf, side=side):
                y_copy(buf, which, side).wait_send()


def eliminate(a):
    n, lanes = a.shape
    full = (8, lanes)
    blocks = [a[8 * i : 8 * i + 8] for i in range(n // 8)]
    sub = lax.broadcasted_iota(jnp.int32, full, 0)
    for p in range(n // 8):
        rest = range(p + 1, n // 8)
        own = blocks[p]

        def column(block, c, p=p):
            return jnp.broadcast_to(block[:, 8 * p + c : 8 * p + c + 1], full)

        rows = [jnp.broadcast_to(own[j : j + 1], full) for j in range(8)]
        own_columns = [column(own, c) for c in range(8)]
        d = {(i, c): jnp.broadcast_to(own_columns[c][i : i + 1], full) for c in range(8) for i in range(c + 1)}
        u = {i: [column(blocks[i], c) for c in range(8)] for i in rest}
        for j in range(8):
            scale = lax.rsqrt(d[j, j])
            rows[j] = rows[j] * scale
            factor = {c: d[j, c] * scale for c in range(j + 1, 8)}
            for c in range(j + 1, 8):
                for e in range(c, 8):
                    d[c, e] = d[c, e] - factor[c] * factor[e]
                rows[c] = rows[c] - factor[c] * rows[j]
            for i in rest:
                u[i][j] = u[i][j] * scale
                for c in range(j + 1, 8):
                    u[i][c] = u[i][c] - u[i][j] * factor[c]
                blocks[i] = blocks[i] - u[i][j] * rows[j]
        done = rows[0]
        for j in range(1, 8):
            done = jnp.where(sub == j, rows[j], done)
        blocks[p] = done
    return jnp.concatenate(blocks, axis=0)


def eye_mask(rows, columns):
    return lax.broadcasted_iota(jnp.int32, (rows, columns), 0) == lax.broadcasted_iota(jnp.int32, (rows, columns), 1)


def dot(a, b):
    return jnp.dot(a, b, precision=HIGHEST, preferred_element_type=F32)


def basis_kernel(root, xs_hbm, g_ref, modes_ref, r_ref, first_ref, xs_ref, out_ref, load_sem, store_sem):
    k = g_ref.shape[0]
    load = pltpu.make_async_copy(xs_hbm, xs_ref, load_sem)
    load.start()
    high, low = g_ref[:, :k], g_ref[:, k:]
    eye = eye_mask(k, k).astype(F32)
    row, column = lax.broadcasted_iota(jnp.int32, (k, k), 0), lax.broadcasted_iota(jnp.int32, (k, k), 1)
    upper = row <= column

    done = eliminate(jnp.concatenate([high, eye], axis=1))
    first = jnp.where(upper, done[:, :k], 0.0).T
    inverse = done[:, k:]
    parts = cut(first)
    first = (parts[2].astype(F32) + parts[1].astype(F32)) + parts[0].astype(F32)
    full, rest = outer_sums(jnp.concatenate(parts, axis=0))
    left = (high - full) + (low - rest)
    gram = eye + dot(dot(inverse, left), inverse.T)

    done = eliminate(jnp.concatenate([gram, eye], axis=1))
    second_t = jnp.where(upper, done[:, :k], 0.0)
    weights = jnp.concatenate([jnp.concatenate([p] * 3, axis=1) for p in cut(dot(done[:, k:], inverse) * root)], axis=0)
    load.wait()
    chunks, lanes = xs_ref.shape[0], out_ref.shape[-1]
    width_x = out_ref.shape[0]
    stores = []
    for x in range(width_x):
        for c in range(chunks):
            prod = jnp.dot(weights, xs_ref[c, :, 2 * lanes * x : 2 * lanes * (x + 1)], preferred_element_type=F32)
            prod = prod[:k] + (prod[k : 2 * k] + prod[2 * k :])
            for i in range(2):
                out_ref[x, :, 2 * c + i, :] = prod[:, i * lanes : (i + 1) * lanes]
        stores.append(pltpu.make_async_copy(out_ref.at[x], modes_ref.at[:, x], store_sem.at[x]))
        stores[-1].start()
    r_ref[...] = dot(second_t, first.T) * (1.0 / root)
    first_ref[...] = first.T * (1.0 / root)
    for store in stores:
        store.wait()


def local(nx, ny, background, sensor_cells, sensor_gain, center, neighbours):
    k, width_x, width_y, lanes = background.shape
    cells = width_x * width_y
    groups = groups_of(nx)
    vmem = pl.BlockSpec(memory_space=pltpu.VMEM)
    dma = pltpu.SemaphoreType.DMA
    slots = max([ny] + [g.size for g in groups])
    rows = k // ny
    pieces_shape = (width_y // 2, 3 * k, 2 * width_x * lanes)
    fields, gram = pl.pallas_call(
        functools.partial(fields_kernel, nx, ny),
        out_shape=(jax.ShapeDtypeStruct(pieces_shape, jnp.bfloat16), jax.ShapeDtypeStruct((k, 2 * k), F32)),
        in_specs=[pl.BlockSpec(memory_space=pltpu.HBM)] * 5,
        out_specs=(pl.BlockSpec(memory_space=pltpu.HBM), vmem),
        scratch_shapes=[
            pltpu.SMEM((k,), jnp.int32),
            pltpu.SMEM((k,), F32),
            pltpu.VMEM((cells, lanes), F32),
            pltpu.VMEM((6, cells, lanes), F32),
            pltpu.VMEM((k * cells, lanes), F32),
            pltpu.VMEM((width_x + 2, width_y + 2, k, lanes), F32),
            pltpu.VMEM((width_x + 2, width_y + 2, k, lanes), F32),
            pltpu.VMEM((cells, k, lanes), F32),
            pltpu.VMEM((k, lanes), jnp.int32),
            pltpu.VMEM((k, lanes), F32),
            pltpu.VMEM(pieces_shape, jnp.bfloat16),
            pltpu.VMEM((k, 2 * k), F32),
            pltpu.VMEM((3, rows, 2 * k), F32),
            pltpu.VMEM((ny, rows, 2 * k), F32),
            pltpu.VMEM((groups[0].size, rows, 2 * k), F32),
            pltpu.VMEM((groups[1].size, rows, 2 * k), F32),
            pltpu.SemaphoreType.REGULAR((3,)), dma((5,)), dma((4,)),
            dma((2, 2, 4)), dma((2, 2, 4)), dma((2, 2)), dma((2, 2)),
            dma((4, slots)), dma((4, slots)),
        ],
        compiler_params=pltpu.CompilerParams(
            collective_id=0, has_side_effects=True, vmem_limit_bytes=56 * 2**20
        ),
        name="fields_and_products",
    )(
        sensor_cells, sensor_gain, background.reshape(k * cells, lanes),
        center.reshape(cells, lanes), neighbours.reshape(6, cells, lanes),
    )
    total_cells = cells * lanes * nx * ny
    root = float(total_cells) ** 0.5
    modes, r_factor, first_r = pl.pallas_call(
        functools.partial(basis_kernel, root),
        out_shape=(
            jax.ShapeDtypeStruct(background.shape, F32),
            jax.ShapeDtypeStruct((k, k), F32),
            jax.ShapeDtypeStruct((k, k), F32),
        ),
        in_specs=[pl.BlockSpec(memory_space=pltpu.HBM), vmem],
        out_specs=(pl.BlockSpec(memory_space=pltpu.HBM), vmem, vmem),
        scratch_shapes=[
            pltpu.VMEM(pieces_shape, jnp.bfloat16), pltpu.VMEM((width_x, k, width_y, lanes), F32), dma, dma((width_x,)),
        ],
        compiler_params=pltpu.CompilerParams(vmem_limit_bytes=56 * 2**20),
        name="basis",
    )(fields, gram)
    return modes, r_factor, first_r


def solution(mesh):
    nx, ny = mesh.shape["gx"], mesh.shape["gy"]
    in_specs = (P(None, "gx", "gy", None), P(), P(), P("gx", "gy", None), P(None, "gx", "gy", None))
    out_specs = (P(None, "gx", "gy", None), P(), P())
    return jax.shard_map(
        functools.partial(local, nx, ny), mesh=mesh, in_specs=in_specs, out_specs=out_specs, check_vma=False
    )
```

```python
import functools

import jax
import jax.numpy as jnp
from jax import lax
from jax.experimental import pallas as pl
from jax.experimental.pallas import tpu as pltpu
from jax.sharding import PartitionSpec as P

MESH = pl.DeviceIdType.MESH
F32 = jnp.float32
HIGHEST = lax.Precision.HIGHEST
ROW_CHUNKS = (0, 3, 1, 2)


def two_sum(a, b):
    s = a + b
    t = s - a
    return s, (a - (s - t)) + (b - t)


def power_below(m):
    q = m * F32(8388609.0)
    return jnp.abs(q - q * F32(0.99999994))


def pieces(s, big):
    first = (s + big) - big
    rest = s - first
    small = big * F32(1.0 / 256)
    second = (rest + small) - small
    return first, second, rest - second


def cut(a):
    big = power_below(jnp.max(jnp.abs(a), axis=1, keepdims=True)) * F32(1.5 * 2**17)
    return [p.astype(jnp.bfloat16) for p in pieces(a, big)]


def outer_sums(stacked):
    n = stacked.shape[0] // 3
    prod = lax.dot_general(stacked, stacked, (((1,), (1,)), ((), ())), preferred_element_type=F32)
    b = [[prod[i * n : (i + 1) * n, j * n : (j + 1) * n] for j in range(3)] for i in range(3)]
    mid, e1 = two_sum(b[0][1], b[1][0])
    high, e2 = two_sum(b[0][0], mid)
    low = ((b[0][2] + b[2][0]) + b[1][1]) + (b[1][2] + b[2][1]) + (e1 + e2)
    return high, low


class Group:
    def __init__(self, axis, digits):
        self.axis, self.digits = axis, digits
        self.size = 1
        for _, count in digits:
            self.size *= count

    def rank(self):
        me = lax.axis_index(self.axis)
        rank = 0
        for stride, count in self.digits:
            rank = rank * count + (me // stride) % count
        return rank

    def member(self, rank):
        me = lax.axis_index(self.axis)
        index = me
        for stride, count in reversed(self.digits):
            index = index + (rank % count - (me // stride) % count) * stride
            rank = rank // count
        return index


def groups_of(size_x):
    if size_x == 64:
        return [Group("gx", [(16, 4), (1, 2)]), Group("gx", [(2, 8)])]
    half = size_x // 2
    return [Group("gx", [(1, 2)]), Group("gx", [(2, half)])]


class Ring:
    def __init__(self, axis, stride, count):
        self.axis, self.stride, self.count = axis, stride, count

    def at(self, distance):
        me = lax.axis_index(self.axis)
        digit = (me // self.stride) % self.count
        steps = sorted({distance % self.count, -distance % self.count} - {0})
        return [{self.axis: me + ((digit + step) % self.count - digit) * self.stride} for step in steps]


def rings_of(nx, ny):
    deep = 16 if nx == 64 else nx
    return Ring("gx", 1, deep), Ring("gx", deep, nx // deep), Ring("gy", 2, ny // 2), Ring("gy", 1, 2)


def sum_slots(buf, count, lanes):
    def body(i, carry):
        total, err = carry
        total, e = two_sum(total, buf[i])
        return total, err + e

    total, err = buf[0], jnp.zeros_like(buf[0])
    for i in range(1, count):
        total, err = body(i, (total, err))
    half = lanes // 2
    low = err + pltpu.roll(total, half, 1)
    high = total + low
    low = low - (high - total)
    lane = lax.broadcasted_iota(jnp.int32, high.shape, 1)
    return jnp.where(lane < half, high, pltpu.roll(low, half, 1))


def fields_kernel(
    nx, ny, cells_hbm, gain_hbm, bg_ref, cen_hbm, nei_hbm, xs_out, g_out,
    cells_ref, gain_ref, cen_ref, nei_ref, bg_v, v_ref, w_ref, s_ref, rel_ref, gains_ref, xs_ref, pack_ref, piece_ref, buf0, buf1, buf2,
    news_sem, own_sem, load_sem, store_sem, x_send, x_recv, y_send, y_recv, r_send, r_recv,
):
    gx, gy = lax.axis_index("gx"), lax.axis_index("gy")
    width_x, width_y, k, lanes = 4, 8, v_ref.shape[2], v_ref.shape[3]
    y_group = Group("gy", [(1, ny)])
    groups = groups_of(nx)
    has_left, has_right = gx > 0, gx < nx - 1
    has_down, has_up = gy > 0, gy < ny - 1

    loads = [
        pltpu.make_async_copy(source, target, load_sem.at[i])
        for i, (source, target) in enumerate((
            (bg_ref, bg_v), (cells_hbm, cells_ref), (gain_hbm, gain_ref), (cen_hbm, cen_ref), (nei_hbm, nei_ref),
        ))
    ]
    for load in loads:
        load.start()

    barrier = pltpu.get_barrier_semaphore()
    rings = rings_of(nx, ny)
    deep = rings[0]
    near = [to for ring in rings for to in ring.at(1)]
    rounds = (near, rings[3].at(1) + Ring("gx", 1, 2).at(1) + deep.at(2), deep.at(4))
    expected = len(near)

    def tell(sem, targets):
        for to in targets:
            pl.semaphore_signal(sem, inc=1, device_id=to, device_id_type=MESH)

    def hear(i):
        if rounds[i]:
            pl.semaphore_wait(news_sem.at[i], len(rounds[i]))

    tell(barrier, near)

    @pl.when(has_left)
    def _():
        pl.semaphore_signal(barrier, inc=1, device_id={"gx": gx - 1}, device_id_type=MESH)

    @pl.when(has_right)
    def _():
        pl.semaphore_signal(barrier, inc=1, device_id={"gx": gx + 1}, device_id_type=MESH)

    for there, to in ((has_down, gy - 1), (has_up, gy + 1)):
        @pl.when(there)
        def _(to=to):
            pl.semaphore_signal(barrier, inc=1, device_id={"gy": to}, device_id_type=MESH)

    zero_plane = jnp.zeros((width_y, k, lanes), F32)
    for edge, row in ((~has_left, 0), (~has_right, width_x + 1)):
        @pl.when(edge)
        def _(row=row):
            v_ref[row, 1 : width_y + 1] = zero_plane
            w_ref[row, 1 : width_y + 1] = zero_plane

    for edge, row in ((~has_down, 0), (~has_up, width_y + 1)):
        @pl.when(edge)
        def _(row=row):
            v_ref[1 : width_x + 1, row] = jnp.zeros((width_x, k, lanes), F32)
            w_ref[1 : width_x + 1, row] = jnp.zeros((width_x, k, lanes), F32)

    sub = lax.broadcasted_iota(jnp.int32, (k, lanes), 0)
    lane = lax.broadcasted_iota(jnp.int32, (k, lanes), 1)

    loads[1].wait()
    loads[2].wait()

    def spread(i, carry):
        cells, gains = carry
        here = sub == i
        return jnp.where(here, cells_ref[i], cells), jnp.where(here, gain_ref[i], gains)

    cells, gains = lax.fori_loop(
        0, k, spread, (jnp.zeros((k, lanes), jnp.int32), jnp.zeros((k, lanes), F32)), unroll=8
    )
    rel_ref[...] = cells - lane
    gains_ref[...] = gains

    loads[0].wait()

    def take(i, _):
        x, y = i // width_y, i % width_y
        at = ((gx * width_x + x) * (width_y * ny) + gy * width_y + y) * lanes
        rows = bg_v[pl.ds(i, k, stride=width_x * width_y), :]
        v_ref[x + 1, y + 1] = rows + jnp.where(rel_ref[...] == at, gains_ref[...], 0.0)
        return 0

    lax.fori_loop(0, width_x * width_y, take, 0, unroll=8)
    for there in (has_left, has_right, has_down, has_up):
        expected = expected + there.astype(jnp.int32)
    pl.semaphore_wait(barrier, expected)

    def x_copy(buf, which, c, side):
        rows = pl.ds(1 + 2 * c, 2)
        source, target = ((1, width_x + 1), (width_x, 0))[side]
        return pltpu.make_async_remote_copy(
            src_ref=buf.at[source, rows], dst_ref=buf.at[target, rows],
            send_sem=x_send.at[which, side, c], recv_sem=x_recv.at[which, side, c],
            device_id={"gx": (gx - 1, gx + 1)[side]}, device_id_type=MESH,
        )

    def y_copy(buf, which, side):
        source, target = ((1, width_y + 1), (width_y, 0))[side]
        planes = pl.ds(1, width_x)
        return pltpu.make_async_remote_copy(
            src_ref=buf.at[planes, source], dst_ref=buf.at[planes, target],
            send_sem=y_send.at[which, side], recv_sem=y_recv.at[which, side],
            device_id={"gy": (gy - 1, gy + 1)[side]}, device_id_type=MESH,
        )

    there_x, there_y = (has_left, has_right), (has_down, has_up)

    def start_x(buf, which, c):
        for side in (0, 1):
            @pl.when(there_x[side])
            def _(side=side):
                x_copy(buf, which, c, side).start()

    def start_y(buf, which, side):
        @pl.when(there_y[side])
        def _():
            y_copy(buf, which, side).start()

    def arrive_x(buf, which, c):
        for side in (0, 1):
            @pl.when(there_x[1 - side])
            def _(side=side):
                x_copy(buf, which, c, side).wait_recv()

    def arrive_y(buf, which, side):
        @pl.when(there_y[1 - side])
        def _():
            y_copy(buf, which, side).wait_recv()

    start_y(v_ref, 0, 0)
    start_y(v_ref, 0, 1)
    for c in ROW_CHUNKS:
        start_x(v_ref, 0, c)
    tell(news_sem.at[0], rounds[0])

    z_lane = lax.broadcasted_iota(jnp.int32, (1, lanes), 1)

    def advance(src, x, y):
        def row(ref):
            return jnp.broadcast_to(ref, (k, lanes))

        i = x * width_y + y
        core = src[x + 1, y + 1]
        upper = jnp.where(z_lane < lanes - 1, nei_ref[4, pl.ds(i, 1), :], 0.0)
        lower = jnp.where(z_lane > 0, nei_ref[5, pl.ds(i, 1), :], 0.0)
        result = row(cen_ref[pl.ds(i, 1), :]) * core
        result = result + row(nei_ref[0, pl.ds(i, 1), :]) * src[x + 2, y + 1]
        result = result + row(nei_ref[1, pl.ds(i, 1), :]) * src[x, y + 1]
        result = result + row(nei_ref[2, pl.ds(i, 1), :]) * src[x + 1, y + 2]
        result = result + row(nei_ref[3, pl.ds(i, 1), :]) * src[x + 1, y]
        result = result + row(upper) * pltpu.roll(core, lanes - 1, 1)
        result = result + row(lower) * pltpu.roll(core, 1, 1)
        return result

    loads[3].wait()
    loads[4].wait()
    arrive_y(v_ref, 0, 0)
    arrive_y(v_ref, 0, 1)
    for c in ROW_CHUNKS:
        arrive_x(v_ref, 0, c)

        def first(i, _, c=c):
            x, y = i // 2, 2 * c + i % 2
            w_ref[x + 1, y + 1] = advance(v_ref, x, y)
            return 0

        lax.fori_loop(0, 2 * width_x, first, 0, unroll=True)
        start_x(w_ref, 1, c)
        if c == 0:
            start_y(w_ref, 1, 0)
        if c == width_y // 2 - 1:
            start_y(w_ref, 1, 1)
        if c == ROW_CHUNKS[0]:
            hear(0)
            tell(news_sem.at[1], rounds[1])
        if c == ROW_CHUNKS[-1]:
            hear(1)
            tell(news_sem.at[2], rounds[2])

    high = jnp.zeros((k, k), F32)
    low = jnp.zeros((k, k), F32)
    for c in ROW_CHUNKS:
        arrive_x(w_ref, 1, c)
        if c == 0:
            arrive_y(w_ref, 1, 1)
        if c == width_y // 2 - 1:
            arrive_y(w_ref, 1, 0)

        def second(i, most, c=c):
            x, y = i // 2, 2 * c + i % 2
            value = advance(w_ref, x, y)
            s_ref[c * 2 * width_x + i] = value
            return jnp.maximum(most, jnp.abs(value))

        most = lax.fori_loop(0, 2 * width_x, second, jnp.zeros((k, lanes), F32), unroll=True)
        big = power_below(jnp.max(most, axis=1, keepdims=True)) * F32(1.5 * 2**17)
        for i in range(2 * width_x):
            for j, piece in enumerate(pieces(s_ref[c * 2 * width_x + i], big)):
                xs_ref[c, j * k : (j + 1) * k, i * lanes : (i + 1) * lanes] = piece.astype(jnp.bfloat16)
        pltpu.make_async_copy(xs_ref.at[c], xs_out.at[c], store_sem.at[c]).start()
        part_high, part_low = outer_sums(xs_ref[c])
        high, e = two_sum(high, part_high)
        low = low + (part_low + e)

    pack_ref[...] = jnp.concatenate([high, low], axis=1)

    rows = k // ny
    y_rank = y_group.rank()

    def share(phase, group, source, target, slot, sem_slot):
        rank = group.rank()
        copies = []
        for step in range(1, group.size):
            peer = (rank + step) % group.size
            copies.append(pltpu.make_async_remote_copy(
                src_ref=source(peer), dst_ref=target(rank),
                send_sem=r_send.at[phase, step], recv_sem=r_recv.at[phase, rank],
                device_id={group.axis: group.member(peer)}, device_id_type=MESH,
            ))
        for copy in copies:
            copy.start()
        return copies

    def gather(phase, group, source, target):
        rank = group.rank()
        for step in range(1, group.size):
            peer = (rank + step) % group.size
            pltpu.make_async_remote_copy(
                src_ref=source(peer), dst_ref=target(peer),
                send_sem=r_send.at[phase, step], recv_sem=r_recv.at[phase, peer],
                device_id={group.axis: group.member(peer)}, device_id_type=MESH,
            ).wait_recv()

    hear(2)
    sent = []

    def part_of(peer):
        return pack_ref.at[pl.ds(pl.multiple_of(peer * rows, rows), rows)]

    buf0[y_rank] = pack_ref[pl.ds(pl.multiple_of(y_rank * rows, rows), rows)]
    sent += share(0, y_group, part_of, lambda r: buf0.at[r], None, None)
    gather(0, y_group, part_of, lambda r: buf0.at[r])
    total = sum_slots(buf0, ny, lanes)
    for phase, (group, buf) in enumerate(zip(groups, (buf1, buf2)), 1):
        here = piece_ref.at[phase - 1]
        here[...] = total
        buf[group.rank()] = total
        sent += share(phase, group, lambda p: here, lambda r: buf.at[r], None, None)
        gather(phase, group, lambda p: here, lambda r: buf.at[r])
        total = sum_slots(buf, group.size, lanes)
    last = piece_ref.at[2]
    last[...] = total

    def rows_of(r):
        return g_out.at[pl.ds(pl.multiple_of(r * rows, rows), rows)]

    own_rows = pltpu.make_async_copy(last, rows_of(y_rank), own_sem)
    own_rows.start()
    sent += share(3, y_group, lambda p: last, rows_of, None, None)
    gather(3, y_group, lambda p: last, rows_of)
    own_rows.wait()

    for copy in sent:
        copy.wait_send()
    for c in ROW_CHUNKS:
        pltpu.make_async_copy(xs_ref.at[c], xs_out.at[c], store_sem.at[c]).wait()
        for which, buf in enumerate((v_ref, w_ref)):
            for side in (0, 1):
                @pl.when(there_x[side])
                def _(c=c, which=which, buf=buf, side=side):
                    x_copy(buf, which, c, side).wait_send()
    for which, buf in enumerate((v_ref, w_ref)):
        for side in (0, 1):
            @pl.when(there_y[side])
            def _(which=which, buf=buf, side=side):
                y_copy(buf, which, side).wait_send()


def eliminate(a):
    n, lanes = a.shape
    full = (8, lanes)
    blocks = [a[8 * i : 8 * i + 8] for i in range(n // 8)]
    sub = lax.broadcasted_iota(jnp.int32, full, 0)
    for p in range(n // 8):
        rest = range(p + 1, n // 8)
        own = blocks[p]

        def column(block, c, p=p):
            return jnp.broadcast_to(block[:, 8 * p + c : 8 * p + c + 1], full)

        rows = [jnp.broadcast_to(own[j : j + 1], full) for j in range(8)]
        own_columns = [column(own, c) for c in range(8)]
        d = {(i, c): jnp.broadcast_to(own_columns[c][i : i + 1], full) for c in range(8) for i in range(c + 1)}
        u = {i: [column(blocks[i], c) for c in range(8)] for i in rest}
        for j in range(8):
            scale = lax.rsqrt(d[j, j])
            rows[j] = rows[j] * scale
            factor = {c: d[j, c] * scale for c in range(j + 1, 8)}
            for c in range(j + 1, 8):
                for e in range(c, 8):
                    d[c, e] = d[c, e] - factor[c] * factor[e]
                rows[c] = rows[c] - factor[c] * rows[j]
            for i in rest:
                u[i][j] = u[i][j] * scale
                for c in range(j + 1, 8):
                    u[i][c] = u[i][c] - u[i][j] * factor[c]
                blocks[i] = blocks[i] - u[i][j] * rows[j]
        done = rows[0]
        for j in range(1, 8):
            done = jnp.where(sub == j, rows[j], done)
        blocks[p] = done
    return jnp.concatenate(blocks, axis=0)


def eye_mask(rows, columns):
    return lax.broadcasted_iota(jnp.int32, (rows, columns), 0) == lax.broadcasted_iota(jnp.int32, (rows, columns), 1)


def dot(a, b):
    return jnp.dot(a, b, precision=HIGHEST, preferred_element_type=F32)


def basis_kernel(root, xs_hbm, g_ref, modes_ref, r_hbm, first_hbm, xs_ref, out_ref, r_ref, first_ref, load_sem, store_sem, small_sem):
    k = g_ref.shape[0]
    load = pltpu.make_async_copy(xs_hbm, xs_ref, load_sem)
    load.start()
    high, low = g_ref[:, :k], g_ref[:, k:]
    eye = eye_mask(k, k).astype(F32)
    row, column = lax.broadcasted_iota(jnp.int32, (k, k), 0), lax.broadcasted_iota(jnp.int32, (k, k), 1)
    upper = row <= column

    done = eliminate(jnp.concatenate([high, eye], axis=1))
    first = jnp.where(upper, done[:, :k], 0.0).T
    inverse = done[:, k:]
    parts = cut(first)
    first = (parts[2].astype(F32) + parts[1].astype(F32)) + parts[0].astype(F32)
    full, rest = outer_sums(jnp.concatenate(parts, axis=0))
    left = (high - full) + (low - rest)
    gram = eye + dot(dot(inverse, left), inverse.T)

    done = eliminate(jnp.concatenate([gram, eye], axis=1))
    second_t = jnp.where(upper, done[:, :k], 0.0)
    weights = jnp.concatenate([jnp.concatenate([p] * 3, axis=1) for p in cut(dot(done[:, k:], inverse) * root)], axis=0)
    load.wait()
    chunks, lanes = xs_ref.shape[0], out_ref.shape[-1]
    width_x = out_ref.shape[0]
    stores = []
    for x in range(width_x):
        for c in range(chunks):
            prod = jnp.dot(weights, xs_ref[c, :, 2 * lanes * x : 2 * lanes * (x + 1)], preferred_element_type=F32)
            prod = prod[:k] + (prod[k : 2 * k] + prod[2 * k :])
            for i in range(2):
                out_ref[x, :, 2 * c + i, :] = prod[:, i * lanes : (i + 1) * lanes]
        stores.append(pltpu.make_async_copy(out_ref.at[x], modes_ref.at[:, x], store_sem.at[x]))
        stores[-1].start()
    small = [
        pltpu.make_async_copy(source, target, small_sem.at[i])
        for i, (source, target) in enumerate(((first_ref, first_hbm), (r_ref, r_hbm)))
    ]
    first_ref[...] = first.T * (1.0 / root)
    small[0].start()
    r_ref[...] = dot(second_t, first.T) * (1.0 / root)
    small[1].start()
    for store in stores + small:
        store.wait()


def local(nx, ny, background, sensor_cells, sensor_gain, center, neighbours):
    k, width_x, width_y, lanes = background.shape
    cells = width_x * width_y
    groups = groups_of(nx)
    vmem = pl.BlockSpec(memory_space=pltpu.VMEM)
    dma = pltpu.SemaphoreType.DMA
    slots = max([ny] + [g.size for g in groups])
    rows = k // ny
    pieces_shape = (width_y // 2, 3 * k, 2 * width_x * lanes)
    fields, gram = pl.pallas_call(
        functools.partial(fields_kernel, nx, ny),
        out_shape=(jax.ShapeDtypeStruct(pieces_shape, jnp.bfloat16), jax.ShapeDtypeStruct((k, 2 * k), F32)),
        in_specs=[pl.BlockSpec(memory_space=pltpu.HBM)] * 5,
        out_specs=(pl.BlockSpec(memory_space=pltpu.HBM), pl.BlockSpec(memory_space=pltpu.HBM)),
        scratch_shapes=[
            pltpu.SMEM((k,), jnp.int32),
            pltpu.SMEM((k,), F32),
            pltpu.VMEM((cells, lanes), F32),
            pltpu.VMEM((6, cells, lanes), F32),
            pltpu.VMEM((k * cells, lanes), F32),
            pltpu.VMEM((width_x + 2, width_y + 2, k, lanes), F32),
            pltpu.VMEM((width_x + 2, width_y + 2, k, lanes), F32),
            pltpu.VMEM((cells, k, lanes), F32),
            pltpu.VMEM((k, lanes), jnp.int32),
            pltpu.VMEM((k, lanes), F32),
            pltpu.VMEM(pieces_shape, jnp.bfloat16),
            pltpu.VMEM((k, 2 * k), F32),
            pltpu.VMEM((3, rows, 2 * k), F32),
            pltpu.VMEM((ny, rows, 2 * k), F32),
            pltpu.VMEM((groups[0].size, rows, 2 * k), F32),
            pltpu.VMEM((groups[1].size, rows, 2 * k), F32),
            pltpu.SemaphoreType.REGULAR((3,)), dma, dma((5,)), dma((4,)),
            dma((2, 2, 4)), dma((2, 2, 4)), dma((2, 2)), dma((2, 2)),
            dma((4, slots)), dma((4, slots)),
        ],
        compiler_params=pltpu.CompilerParams(
            collective_id=0, has_side_effects=True, vmem_limit_bytes=56 * 2**20
        ),
        name="fields_and_products",
    )(
        sensor_cells, sensor_gain, background.reshape(k * cells, lanes),
        center.reshape(cells, lanes), neighbours.reshape(6, cells, lanes),
    )
    total_cells = cells * lanes * nx * ny
    root = float(total_cells) ** 0.5
    modes, r_factor, first_r = pl.pallas_call(
        functools.partial(basis_kernel, root),
        out_shape=(
            jax.ShapeDtypeStruct(background.shape, F32),
            jax.ShapeDtypeStruct((k, k), F32),
            jax.ShapeDtypeStruct((k, k), F32),
        ),
        in_specs=[pl.BlockSpec(memory_space=pltpu.HBM), vmem],
        out_specs=(pl.BlockSpec(memory_space=pltpu.HBM),) * 3,
        scratch_shapes=[
            pltpu.VMEM(pieces_shape, jnp.bfloat16), pltpu.VMEM((width_x, k, width_y, lanes), F32),
            pltpu.VMEM((k, k), F32), pltpu.VMEM((k, k), F32), dma, dma((width_x,)), dma((2,)),
        ],
        compiler_params=pltpu.CompilerParams(vmem_limit_bytes=56 * 2**20),
        name="basis",
    )(fields, gram)
    return modes, r_factor, first_r


def solution(mesh):
    nx, ny = mesh.shape["gx"], mesh.shape["gy"]
    in_specs = (P(None, "gx", "gy", None), P(), P(), P("gx", "gy", None), P(None, "gx", "gy", None))
    out_specs = (P(None, "gx", "gy", None), P(), P())
    return jax.shard_map(
        functools.partial(local, nx, ny), mesh=mesh, in_specs=in_specs, out_specs=out_specs, check_vma=False
    )
```

```python
import functools

import jax
import jax.numpy as jnp
from jax import lax
from jax.experimental import pallas as pl
from jax.experimental.pallas import tpu as pltpu
from jax.sharding import PartitionSpec as P

MESH = pl.DeviceIdType.MESH
F32 = jnp.float32
HIGHEST = lax.Precision.HIGHEST
ROW_CHUNKS = (0, 3, 1, 2)


def two_sum(a, b):
    s = a + b
    t = s - a
    return s, (a - (s - t)) + (b - t)


def power_below(m):
    q = m * F32(8388609.0)
    return jnp.abs(q - q * F32(0.99999994))


def pieces(s, big):
    first = (s + big) - big
    rest = s - first
    small = big * F32(1.0 / 256)
    second = (rest + small) - small
    return first, second, rest - second


def cut(a):
    big = power_below(jnp.max(jnp.abs(a), axis=1, keepdims=True)) * F32(1.5 * 2**17)
    return [p.astype(jnp.bfloat16) for p in pieces(a, big)]


def outer_sums(stacked):
    n = stacked.shape[0] // 3
    prod = lax.dot_general(stacked, stacked, (((1,), (1,)), ((), ())), preferred_element_type=F32)
    b = [[prod[i * n : (i + 1) * n, j * n : (j + 1) * n] for j in range(3)] for i in range(3)]
    mid, e1 = two_sum(b[0][1], b[1][0])
    high, e2 = two_sum(b[0][0], mid)
    low = ((b[0][2] + b[2][0]) + b[1][1]) + (b[1][2] + b[2][1]) + (e1 + e2)
    return high, low


class Group:
    def __init__(self, axis, digits):
        self.axis, self.digits = axis, digits
        self.size = 1
        for _, count in digits:
            self.size *= count

    def rank(self):
        me = lax.axis_index(self.axis)
        rank = 0
        for stride, count in self.digits:
            rank = rank * count + (me // stride) % count
        return rank

    def member(self, rank):
        me = lax.axis_index(self.axis)
        index = me
        for stride, count in reversed(self.digits):
            index = index + (rank % count - (me // stride) % count) * stride
            rank = rank // count
        return index


def groups_of(size_x):
    if size_x == 64:
        return [Group("gx", [(16, 4), (1, 2)]), Group("gx", [(2, 8)])]
    half = size_x // 2
    return [Group("gx", [(1, 2)]), Group("gx", [(2, half)])]


def far_first(size):
    return sorted(range(1, size), key=lambda step: -min(step, size - step))


class Ring:
    def __init__(self, axis, stride, count):
        self.axis, self.stride, self.count = axis, stride, count

    def at(self, distance):
        me = lax.axis_index(self.axis)
        digit = (me // self.stride) % self.count
        steps = sorted({distance % self.count, -distance % self.count} - {0})
        return [{self.axis: me + ((digit + step) % self.count - digit) * self.stride} for step in steps]


def rings_of(nx, ny):
    deep = 16 if nx == 64 else nx
    return Ring("gx", 1, deep), Ring("gx", deep, nx // deep), Ring("gy", 2, ny // 2), Ring("gy", 1, 2)


def sum_slots(buf, count, lanes):
    totals, err = [buf[i] for i in range(count)], jnp.zeros_like(buf[0])
    while len(totals) > 1:
        pairs = [two_sum(a, b) for a, b in zip(totals[::2], totals[1::2])]
        totals = [total for total, _ in pairs]
        for _, e in pairs:
            err = err + e
    total = totals[0]
    half = lanes // 2
    low = err + pltpu.roll(total, half, 1)
    high = total + low
    low = low - (high - total)
    lane = lax.broadcasted_iota(jnp.int32, high.shape, 1)
    return jnp.where(lane < half, high, pltpu.roll(low, half, 1))


def fields_kernel(
    nx, ny, cells_hbm, gain_hbm, bg_ref, cen_hbm, nei_hbm, xs_out, g_out,
    cells_ref, gain_ref, cen_ref, nei_ref, bg_v, v_ref, w_ref, s_ref, rel_ref, gains_ref, xs_ref, pack_ref, piece_ref, buf0, buf1, buf2,
    news_sem, own_sem, load_sem, store_sem, x_send, x_recv, y_send, y_recv, r_send, r_recv,
):
    gx, gy = lax.axis_index("gx"), lax.axis_index("gy")
    width_x, width_y, k, lanes = 4, 8, v_ref.shape[2], v_ref.shape[3]
    y_group = Group("gy", [(1, ny)])
    groups = groups_of(nx)
    has_left, has_right = gx > 0, gx < nx - 1
    has_down, has_up = gy > 0, gy < ny - 1

    loads = [
        pltpu.make_async_copy(source, target, load_sem.at[i])
        for i, (source, target) in enumerate((
            (bg_ref, bg_v), (cells_hbm, cells_ref), (gain_hbm, gain_ref), (cen_hbm, cen_ref), (nei_hbm, nei_ref),
        ))
    ]
    for load in loads:
        load.start()

    barrier = pltpu.get_barrier_semaphore()
    rings = rings_of(nx, ny)
    deep = rings[0]
    near = [to for ring in rings for to in ring.at(1)]
    rounds = (near, rings[3].at(1) + Ring("gx", 1, 2).at(1) + deep.at(2), deep.at(4))
    expected = len(near)

    def tell(sem, targets):
        for to in targets:
            pl.semaphore_signal(sem, inc=1, device_id=to, device_id_type=MESH)

    def hear(i):
        if rounds[i]:
            pl.semaphore_wait(news_sem.at[i], len(rounds[i]))

    tell(barrier, near)

    @pl.when(has_left)
    def _():
        pl.semaphore_signal(barrier, inc=1, device_id={"gx": gx - 1}, device_id_type=MESH)

    @pl.when(has_right)
    def _():
        pl.semaphore_signal(barrier, inc=1, device_id={"gx": gx + 1}, device_id_type=MESH)

    for there, to in ((has_down, gy - 1), (has_up, gy + 1)):
        @pl.when(there)
        def _(to=to):
            pl.semaphore_signal(barrier, inc=1, device_id={"gy": to}, device_id_type=MESH)

    zero_plane = jnp.zeros((width_y, k, lanes), F32)
    for edge, row in ((~has_left, 0), (~has_right, width_x + 1)):
        @pl.when(edge)
        def _(row=row):
            v_ref[row, 1 : width_y + 1] = zero_plane
            w_ref[row, 1 : width_y + 1] = zero_plane

    for edge, row in ((~has_down, 0), (~has_up, width_y + 1)):
        @pl.when(edge)
        def _(row=row):
            v_ref[1 : width_x + 1, row] = jnp.zeros((width_x, k, lanes), F32)
            w_ref[1 : width_x + 1, row] = jnp.zeros((width_x, k, lanes), F32)

    sub = lax.broadcasted_iota(jnp.int32, (k, lanes), 0)
    lane = lax.broadcasted_iota(jnp.int32, (k, lanes), 1)

    loads[1].wait()
    loads[2].wait()

    def spread(i, carry):
        cells, gains = carry
        here = sub == i
        return jnp.where(here, cells_ref[i], cells), jnp.where(here, gain_ref[i], gains)

    cells, gains = lax.fori_loop(
        0, k, spread, (jnp.zeros((k, lanes), jnp.int32), jnp.zeros((k, lanes), F32)), unroll=8
    )
    rel_ref[...] = cells - lane
    gains_ref[...] = gains

    loads[0].wait()

    def take(i, _):
        x, y = i // width_y, i % width_y
        at = ((gx * width_x + x) * (width_y * ny) + gy * width_y + y) * lanes
        rows = bg_v[pl.ds(i, k, stride=width_x * width_y), :]
        v_ref[x + 1, y + 1] = rows + jnp.where(rel_ref[...] == at, gains_ref[...], 0.0)
        return 0

    lax.fori_loop(0, width_x * width_y, take, 0, unroll=8)
    for there in (has_left, has_right, has_down, has_up):
        expected = expected + there.astype(jnp.int32)
    pl.semaphore_wait(barrier, expected)

    def x_copy(buf, which, c, side):
        rows = pl.ds(1 + 2 * c, 2)
        source, target = ((1, width_x + 1), (width_x, 0))[side]
        return pltpu.make_async_remote_copy(
            src_ref=buf.at[source, rows], dst_ref=buf.at[target, rows],
            send_sem=x_send.at[which, side, c], recv_sem=x_recv.at[which, side, c],
            device_id={"gx": (gx - 1, gx + 1)[side]}, device_id_type=MESH,
        )

    def y_copy(buf, which, side):
        source, target = ((1, width_y + 1), (width_y, 0))[side]
        planes = pl.ds(1, width_x)
        return pltpu.make_async_remote_copy(
            src_ref=buf.at[planes, source], dst_ref=buf.at[planes, target],
            send_sem=y_send.at[which, side], recv_sem=y_recv.at[which, side],
            device_id={"gy": (gy - 1, gy + 1)[side]}, device_id_type=MESH,
        )

    there_x, there_y = (has_left, has_right), (has_down, has_up)

    def start_x(buf, which, c):
        for side in (0, 1):
            @pl.when(there_x[side])
            def _(side=side):
                x_copy(buf, which, c, side).start()

    def start_y(buf, which, side):
        @pl.when(there_y[side])
        def _():
            y_copy(buf, which, side).start()

    def arrive_x(buf, which, c):
        for side in (0, 1):
            @pl.when(there_x[1 - side])
            def _(side=side):
                x_copy(buf, which, c, side).wait_recv()

    def arrive_y(buf, which, side):
        @pl.when(there_y[1 - side])
        def _():
            y_copy(buf, which, side).wait_recv()

    start_y(v_ref, 0, 0)
    start_y(v_ref, 0, 1)
    for c in ROW_CHUNKS:
        start_x(v_ref, 0, c)
    tell(news_sem.at[0], rounds[0])

    z_lane = lax.broadcasted_iota(jnp.int32, (1, lanes), 1)

    def advance(src, x, y):
        def row(ref):
            return jnp.broadcast_to(ref, (k, lanes))

        i = x * width_y + y
        core = src[x + 1, y + 1]
        upper = jnp.where(z_lane < lanes - 1, nei_ref[4, pl.ds(i, 1), :], 0.0)
        lower = jnp.where(z_lane > 0, nei_ref[5, pl.ds(i, 1), :], 0.0)
        result = row(cen_ref[pl.ds(i, 1), :]) * core
        result = result + row(nei_ref[0, pl.ds(i, 1), :]) * src[x + 2, y + 1]
        result = result + row(nei_ref[1, pl.ds(i, 1), :]) * src[x, y + 1]
        result = result + row(nei_ref[2, pl.ds(i, 1), :]) * src[x + 1, y + 2]
        result = result + row(nei_ref[3, pl.ds(i, 1), :]) * src[x + 1, y]
        result = result + row(upper) * pltpu.roll(core, lanes - 1, 1)
        result = result + row(lower) * pltpu.roll(core, 1, 1)
        return result

    loads[3].wait()
    loads[4].wait()
    arrive_y(v_ref, 0, 0)
    arrive_y(v_ref, 0, 1)
    for c in ROW_CHUNKS:
        arrive_x(v_ref, 0, c)

        def first(i, _, c=c):
            x, y = i // 2, 2 * c + i % 2
            w_ref[x + 1, y + 1] = advance(v_ref, x, y)
            return 0

        lax.fori_loop(0, 2 * width_x, first, 0, unroll=True)
        start_x(w_ref, 1, c)
        if c == 0:
            start_y(w_ref, 1, 0)
        if c == width_y // 2 - 1:
            start_y(w_ref, 1, 1)
        if c == ROW_CHUNKS[0]:
            hear(0)
            tell(news_sem.at[1], rounds[1])
        if c == ROW_CHUNKS[-1]:
            hear(1)
            tell(news_sem.at[2], rounds[2])

    high = jnp.zeros((k, k), F32)
    low = jnp.zeros((k, k), F32)
    for c in ROW_CHUNKS:
        arrive_x(w_ref, 1, c)
        if c == 0:
            arrive_y(w_ref, 1, 1)
        if c == width_y // 2 - 1:
            arrive_y(w_ref, 1, 0)

        def second(i, most, c=c):
            x, y = i // 2, 2 * c + i % 2
            value = advance(w_ref, x, y)
            s_ref[c * 2 * width_x + i] = value
            return jnp.maximum(most, jnp.abs(value))

        most = lax.fori_loop(0, 2 * width_x, second, jnp.zeros((k, lanes), F32), unroll=True)
        big = power_below(jnp.max(most, axis=1, keepdims=True)) * F32(1.5 * 2**17)
        for i in range(2 * width_x):
            for j, piece in enumerate(pieces(s_ref[c * 2 * width_x + i], big)):
                xs_ref[c, j * k : (j + 1) * k, i * lanes : (i + 1) * lanes] = piece.astype(jnp.bfloat16)
        pltpu.make_async_copy(xs_ref.at[c], xs_out.at[c], store_sem.at[c]).start()
        part_high, part_low = outer_sums(xs_ref[c])
        high, e = two_sum(high, part_high)
        low = low + (part_low + e)

    pack_ref[...] = jnp.concatenate([high, low], axis=1)

    rows = k // ny
    y_rank = y_group.rank()

    def share(phase, group, source, target, slot, sem_slot):
        rank = group.rank()
        copies = []
        for step in far_first(group.size):
            peer = (rank + step) % group.size
            copies.append(pltpu.make_async_remote_copy(
                src_ref=source(peer), dst_ref=target(rank),
                send_sem=r_send.at[phase, step], recv_sem=r_recv.at[phase, rank],
                device_id={group.axis: group.member(peer)}, device_id_type=MESH,
            ))
        for copy in copies:
            copy.start()
        return copies

    def gather(phase, group, source, target):
        rank = group.rank()
        for step in range(1, group.size):
            peer = (rank + step) % group.size
            pltpu.make_async_remote_copy(
                src_ref=source(peer), dst_ref=target(peer),
                send_sem=r_send.at[phase, step], recv_sem=r_recv.at[phase, peer],
                device_id={group.axis: group.member(peer)}, device_id_type=MESH,
            ).wait_recv()

    hear(2)
    sent = []

    def part_of(peer):
        return pack_ref.at[pl.ds(pl.multiple_of(peer * rows, rows), rows)]

    buf0[y_rank] = pack_ref[pl.ds(pl.multiple_of(y_rank * rows, rows), rows)]
    sent += share(0, y_group, part_of, lambda r: buf0.at[r], None, None)
    gather(0, y_group, part_of, lambda r: buf0.at[r])
    total = sum_slots(buf0, ny, lanes)
    for phase, (group, buf) in enumerate(zip(groups, (buf1, buf2)), 1):
        here = piece_ref.at[phase - 1]
        here[...] = total
        buf[group.rank()] = total
        sent += share(phase, group, lambda p: here, lambda r: buf.at[r], None, None)
        gather(phase, group, lambda p: here, lambda r: buf.at[r])
        total = sum_slots(buf, group.size, lanes)
    last = piece_ref.at[2]
    last[...] = total

    def rows_of(r):
        return g_out.at[pl.ds(pl.multiple_of(r * rows, rows), rows)]

    own_rows = pltpu.make_async_copy(last, rows_of(y_rank), own_sem)
    own_rows.start()
    sent += share(3, y_group, lambda p: last, rows_of, None, None)
    gather(3, y_group, lambda p: last, rows_of)
    own_rows.wait()

    for copy in sent:
        copy.wait_send()
    for c in ROW_CHUNKS:
        pltpu.make_async_copy(xs_ref.at[c], xs_out.at[c], store_sem.at[c]).wait()
        for which, buf in enumerate((v_ref, w_ref)):
            for side in (0, 1):
                @pl.when(there_x[side])
                def _(c=c, which=which, buf=buf, side=side):
                    x_copy(buf, which, c, side).wait_send()
    for which, buf in enumerate((v_ref, w_ref)):
        for side in (0, 1):
            @pl.when(there_y[side])
            def _(which=which, buf=buf, side=side):
                y_copy(buf, which, side).wait_send()


def eliminate(a):
    n, lanes = a.shape
    full = (8, lanes)
    blocks = [a[8 * i : 8 * i + 8] for i in range(n // 8)]
    sub = lax.broadcasted_iota(jnp.int32, full, 0)
    for p in range(n // 8):
        rest = range(p + 1, n // 8)
        own = blocks[p]

        def column(block, c, p=p):
            return jnp.broadcast_to(block[:, 8 * p + c : 8 * p + c + 1], full)

        rows = [jnp.broadcast_to(own[j : j + 1], full) for j in range(8)]
        own_columns = [column(own, c) for c in range(8)]
        d = {(i, c): jnp.broadcast_to(own_columns[c][i : i + 1], full) for c in range(8) for i in range(c + 1)}
        u = {i: [column(blocks[i], c) for c in range(8)] for i in rest}
        for j in range(8):
            scale = lax.rsqrt(d[j, j])
            rows[j] = rows[j] * scale
            factor = {c: d[j, c] * scale for c in range(j + 1, 8)}
            for c in range(j + 1, 8):
                for e in range(c, 8):
                    d[c, e] = d[c, e] - factor[c] * factor[e]
                rows[c] = rows[c] - factor[c] * rows[j]
            for i in rest:
                u[i][j] = u[i][j] * scale
                for c in range(j + 1, 8):
                    u[i][c] = u[i][c] - u[i][j] * factor[c]
                blocks[i] = blocks[i] - u[i][j] * rows[j]
        done = rows[0]
        for j in range(1, 8):
            done = jnp.where(sub == j, rows[j], done)
        blocks[p] = done
    return jnp.concatenate(blocks, axis=0)


def eye_mask(rows, columns):
    return lax.broadcasted_iota(jnp.int32, (rows, columns), 0) == lax.broadcasted_iota(jnp.int32, (rows, columns), 1)


def dot(a, b):
    return jnp.dot(a, b, precision=HIGHEST, preferred_element_type=F32)


def basis_kernel(root, xs_hbm, g_ref, modes_ref, r_hbm, first_hbm, xs_ref, out_ref, r_ref, first_ref, load_sem, store_sem, small_sem):
    k = g_ref.shape[0]
    load = pltpu.make_async_copy(xs_hbm, xs_ref, load_sem)
    load.start()
    high, low = g_ref[:, :k], g_ref[:, k:]
    eye = eye_mask(k, k).astype(F32)
    row, column = lax.broadcasted_iota(jnp.int32, (k, k), 0), lax.broadcasted_iota(jnp.int32, (k, k), 1)
    upper = row <= column

    done = eliminate(jnp.concatenate([high, eye], axis=1))
    first = jnp.where(upper, done[:, :k], 0.0).T
    inverse = done[:, k:]
    parts = cut(first)
    first = (parts[2].astype(F32) + parts[1].astype(F32)) + parts[0].astype(F32)
    full, rest = outer_sums(jnp.concatenate(parts, axis=0))
    left = (high - full) + (low - rest)
    gram = eye + dot(dot(inverse, left), inverse.T)

    done = eliminate(jnp.concatenate([gram, eye], axis=1))
    second_t = jnp.where(upper, done[:, :k], 0.0)
    weights = jnp.concatenate([jnp.concatenate([p] * 3, axis=1) for p in cut(dot(done[:, k:], inverse) * root)], axis=0)
    load.wait()
    chunks, lanes = xs_ref.shape[0], out_ref.shape[-1]
    width_x, _, width_y, _ = out_ref.shape
    flat = out_ref.reshape(width_x, k * width_y, lanes)
    stores = []
    for x in range(width_x):
        for c in range(chunks):
            prod = jnp.dot(weights, xs_ref[c, :, 2 * lanes * x : 2 * lanes * (x + 1)], preferred_element_type=F32)
            prod = prod[:k] + (prod[k : 2 * k] + prod[2 * k :])
            for i in range(2):
                flat[x, pl.ds(2 * c + i, k, stride=width_y), :] = prod[:, i * lanes : (i + 1) * lanes]
        stores.append(pltpu.make_async_copy(out_ref.at[x], modes_ref.at[:, x], store_sem.at[x]))
        stores[-1].start()
    small = [
        pltpu.make_async_copy(source, target, small_sem.at[i])
        for i, (source, target) in enumerate(((first_ref, first_hbm), (r_ref, r_hbm)))
    ]
    first_ref[...] = first.T * (1.0 / root)
    small[0].start()
    r_ref[...] = dot(second_t, first.T) * (1.0 / root)
    small[1].start()
    for store in stores + small:
        store.wait()


def local(nx, ny, background, sensor_cells, sensor_gain, center, neighbours):
    k, width_x, width_y, lanes = background.shape
    cells = width_x * width_y
    groups = groups_of(nx)
    vmem = pl.BlockSpec(memory_space=pltpu.VMEM)
    dma = pltpu.SemaphoreType.DMA
    slots = max([ny] + [g.size for g in groups])
    rows = k // ny
    pieces_shape = (width_y // 2, 3 * k, 2 * width_x * lanes)
    fields, gram = pl.pallas_call(
        functools.partial(fields_kernel, nx, ny),
        out_shape=(jax.ShapeDtypeStruct(pieces_shape, jnp.bfloat16), jax.ShapeDtypeStruct((k, 2 * k), F32)),
        in_specs=[pl.BlockSpec(memory_space=pltpu.HBM)] * 5,
        out_specs=(pl.BlockSpec(memory_space=pltpu.HBM), pl.BlockSpec(memory_space=pltpu.HBM)),
        scratch_shapes=[
            pltpu.SMEM((k,), jnp.int32),
            pltpu.SMEM((k,), F32),
            pltpu.VMEM((cells, lanes), F32),
            pltpu.VMEM((6, cells, lanes), F32),
            pltpu.VMEM((k * cells, lanes), F32),
            pltpu.VMEM((width_x + 2, width_y + 2, k, lanes), F32),
            pltpu.VMEM((width_x + 2, width_y + 2, k, lanes), F32),
            pltpu.VMEM((cells, k, lanes), F32),
            pltpu.VMEM((k, lanes), jnp.int32),
            pltpu.VMEM((k, lanes), F32),
            pltpu.VMEM(pieces_shape, jnp.bfloat16),
            pltpu.VMEM((k, 2 * k), F32),
            pltpu.VMEM((3, rows, 2 * k), F32),
            pltpu.VMEM((ny, rows, 2 * k), F32),
            pltpu.VMEM((groups[0].size, rows, 2 * k), F32),
            pltpu.VMEM((groups[1].size, rows, 2 * k), F32),
            pltpu.SemaphoreType.REGULAR((3,)), dma, dma((5,)), dma((4,)),
            dma((2, 2, 4)), dma((2, 2, 4)), dma((2, 2)), dma((2, 2)),
            dma((4, slots)), dma((4, slots)),
        ],
        compiler_params=pltpu.CompilerParams(
            collective_id=0, has_side_effects=True, vmem_limit_bytes=56 * 2**20
        ),
        name="fields_and_products",
    )(
        sensor_cells, sensor_gain, background.reshape(k * cells, lanes),
        center.reshape(cells, lanes), neighbours.reshape(6, cells, lanes),
    )
    total_cells = cells * lanes * nx * ny
    root = float(total_cells) ** 0.5
    modes, r_factor, first_r = pl.pallas_call(
        functools.partial(basis_kernel, root),
        out_shape=(
            jax.ShapeDtypeStruct(background.shape, F32),
            jax.ShapeDtypeStruct((k, k), F32),
            jax.ShapeDtypeStruct((k, k), F32),
        ),
        in_specs=[pl.BlockSpec(memory_space=pltpu.HBM), vmem],
        out_specs=(pl.BlockSpec(memory_space=pltpu.HBM),) * 3,
        scratch_shapes=[
            pltpu.VMEM(pieces_shape, jnp.bfloat16), pltpu.VMEM((width_x, k, width_y, lanes), F32),
            pltpu.VMEM((k, k), F32), pltpu.VMEM((k, k), F32), dma, dma((width_x,)), dma((2,)),
        ],
        compiler_params=pltpu.CompilerParams(vmem_limit_bytes=56 * 2**20),
        name="basis",
    )(fields, gram)
    return modes, r_factor, first_r


def solution(mesh):
    nx, ny = mesh.shape["gx"], mesh.shape["gy"]
    in_specs = (P(None, "gx", "gy", None), P(), P(), P("gx", "gy", None), P(None, "gx", "gy", None))
    out_specs = (P(None, "gx", "gy", None), P(), P())
    return jax.shard_map(
        functools.partial(local, nx, ny), mesh=mesh, in_specs=in_specs, out_specs=out_specs, check_vma=False
    )
```

```python
import functools

import jax
import jax.numpy as jnp
from jax import lax
from jax.experimental import pallas as pl
from jax.experimental.pallas import tpu as pltpu
from jax.sharding import PartitionSpec as P

MESH = pl.DeviceIdType.MESH
F32 = jnp.float32
HIGHEST = lax.Precision.HIGHEST
ROW_CHUNKS = (0, 3, 1, 2)


def two_sum(a, b):
    s = a + b
    t = s - a
    return s, (a - (s - t)) + (b - t)


def power_below(m):
    q = m * F32(8388609.0)
    return jnp.abs(q - q * F32(0.99999994))


def pieces(s, big):
    first = (s + big) - big
    rest = s - first
    small = big * F32(1.0 / 256)
    second = (rest + small) - small
    return first, second, rest - second


def cut(a):
    big = power_below(jnp.max(jnp.abs(a), axis=1, keepdims=True)) * F32(1.5 * 2**17)
    return [p.astype(jnp.bfloat16) for p in pieces(a, big)]


def outer_sums(stacked):
    n = stacked.shape[0] // 3
    prod = lax.dot_general(stacked, stacked, (((1,), (1,)), ((), ())), preferred_element_type=F32)
    b = [[prod[i * n : (i + 1) * n, j * n : (j + 1) * n] for j in range(3)] for i in range(3)]
    mid, e1 = two_sum(b[0][1], b[1][0])
    high, e2 = two_sum(b[0][0], mid)
    low = ((b[0][2] + b[2][0]) + b[1][1]) + (b[1][2] + b[2][1]) + (e1 + e2)
    return high, low


class Group:
    def __init__(self, axis, digits):
        self.axis, self.digits = axis, digits
        self.size = 1
        for _, count in digits:
            self.size *= count

    def rank(self):
        me = lax.axis_index(self.axis)
        rank = 0
        for stride, count in self.digits:
            rank = rank * count + (me // stride) % count
        return rank

    def member(self, rank):
        me = lax.axis_index(self.axis)
        index = me
        for stride, count in reversed(self.digits):
            index = index + (rank % count - (me // stride) % count) * stride
            rank = rank // count
        return index


def groups_of(size_x):
    if size_x == 64:
        return [Group("gx", [(16, 4), (1, 2)]), Group("gx", [(2, 8)])]
    half = size_x // 2
    return [Group("gx", [(1, 2)]), Group("gx", [(2, half)])]


def far_first(size):
    return sorted(range(1, size), key=lambda step: -min(step, size - step))


class Ring:
    def __init__(self, axis, stride, count):
        self.axis, self.stride, self.count = axis, stride, count

    def at(self, distance):
        me = lax.axis_index(self.axis)
        digit = (me // self.stride) % self.count
        steps = sorted({distance % self.count, -distance % self.count} - {0})
        return [{self.axis: me + ((digit + step) % self.count - digit) * self.stride} for step in steps]


def rings_of(nx, ny):
    deep = 16 if nx == 64 else nx
    return Ring("gx", 1, deep), Ring("gx", deep, nx // deep), Ring("gy", 2, ny // 2), Ring("gy", 1, 2)


def sum_slots(buf, count, lanes):
    totals, err = [buf[i] for i in range(count)], jnp.zeros_like(buf[0])
    while len(totals) > 1:
        pairs = [two_sum(a, b) for a, b in zip(totals[::2], totals[1::2])]
        totals = [total for total, _ in pairs]
        for _, e in pairs:
            err = err + e
    total = totals[0]
    half = lanes // 2
    low = err + pltpu.roll(total, half, 1)
    high = total + low
    low = low - (high - total)
    lane = lax.broadcasted_iota(jnp.int32, high.shape, 1)
    return jnp.where(lane < half, high, pltpu.roll(low, half, 1))


def fields_kernel(
    nx, ny, cells_hbm, gain_hbm, bg_ref, cen_hbm, nei_hbm, xs_out, g_out,
    cells_ref, gain_ref, cen_ref, nei_ref, bg_v, v_ref, w_ref, s_ref, rel_ref, gains_ref, xs_ref, pack_ref, piece_ref, buf0, buf1, buf2,
    news_sem, own_sem, load_sem, store_sem, x_send, x_recv, y_send, y_recv, r_send, r_recv,
):
    gx, gy = lax.axis_index("gx"), lax.axis_index("gy")
    width_x, width_y, k, lanes = 4, 8, v_ref.shape[2], v_ref.shape[3]
    y_group = Group("gy", [(1, ny)])
    groups = groups_of(nx)
    has_left, has_right = gx > 0, gx < nx - 1
    has_down, has_up = gy > 0, gy < ny - 1

    loads = [
        pltpu.make_async_copy(source, target, load_sem.at[i])
        for i, (source, target) in enumerate((
            (bg_ref, bg_v), (cells_hbm, cells_ref), (gain_hbm, gain_ref), (cen_hbm, cen_ref), (nei_hbm, nei_ref),
        ))
    ]
    for load in loads:
        load.start()

    barrier = pltpu.get_barrier_semaphore()
    rings = rings_of(nx, ny)
    deep = rings[0]
    near = [to for ring in rings for to in ring.at(1)]
    rounds = (near, rings[3].at(1) + Ring("gx", 1, 2).at(1) + deep.at(2), deep.at(4))
    expected = len(near)

    def tell(sem, targets):
        for to in targets:
            pl.semaphore_signal(sem, inc=1, device_id=to, device_id_type=MESH)

    def hear(i):
        if rounds[i]:
            pl.semaphore_wait(news_sem.at[i], len(rounds[i]))

    tell(barrier, near)

    @pl.when(has_left)
    def _():
        pl.semaphore_signal(barrier, inc=1, device_id={"gx": gx - 1}, device_id_type=MESH)

    @pl.when(has_right)
    def _():
        pl.semaphore_signal(barrier, inc=1, device_id={"gx": gx + 1}, device_id_type=MESH)

    for there, to in ((has_down, gy - 1), (has_up, gy + 1)):
        @pl.when(there)
        def _(to=to):
            pl.semaphore_signal(barrier, inc=1, device_id={"gy": to}, device_id_type=MESH)

    zero_plane = jnp.zeros((width_y, k, lanes), F32)
    for edge, row in ((~has_left, 0), (~has_right, width_x + 1)):
        @pl.when(edge)
        def _(row=row):
            v_ref[row, 1 : width_y + 1] = zero_plane
            w_ref[row, 1 : width_y + 1] = zero_plane

    for edge, row in ((~has_down, 0), (~has_up, width_y + 1)):
        @pl.when(edge)
        def _(row=row):
            v_ref[1 : width_x + 1, row] = jnp.zeros((width_x, k, lanes), F32)
            w_ref[1 : width_x + 1, row] = jnp.zeros((width_x, k, lanes), F32)

    sub = lax.broadcasted_iota(jnp.int32, (k, lanes), 0)
    lane = lax.broadcasted_iota(jnp.int32, (k, lanes), 1)

    loads[1].wait()
    loads[2].wait()

    def spread(i, carry):
        cells, gains = carry
        here = sub == i
        return jnp.where(here, cells_ref[i], cells), jnp.where(here, gain_ref[i], gains)

    cells, gains = lax.fori_loop(
        0, k, spread, (jnp.zeros((k, lanes), jnp.int32), jnp.zeros((k, lanes), F32)), unroll=8
    )
    rel_ref[...] = cells - lane
    gains_ref[...] = gains

    loads[0].wait()

    def take(i, _):
        x, y = i // width_y, i % width_y
        at = ((gx * width_x + x) * (width_y * ny) + gy * width_y + y) * lanes
        rows = bg_v[pl.ds(i, k, stride=width_x * width_y), :]
        v_ref[x + 1, y + 1] = rows + jnp.where(rel_ref[...] == at, gains_ref[...], 0.0)
        return 0

    lax.fori_loop(0, width_x * width_y, take, 0, unroll=8)
    for there in (has_left, has_right, has_down, has_up):
        expected = expected + there.astype(jnp.int32)
    pl.semaphore_wait(barrier, expected)

    def x_copy(buf, which, c, side):
        rows = pl.ds(1 + 2 * c, 2)
        source, target = ((1, width_x + 1), (width_x, 0))[side]
        return pltpu.make_async_remote_copy(
            src_ref=buf.at[source, rows], dst_ref=buf.at[target, rows],
            send_sem=x_send.at[which, side, c], recv_sem=x_recv.at[which, side, c],
            device_id={"gx": (gx - 1, gx + 1)[side]}, device_id_type=MESH,
        )

    def y_copy(buf, which, side):
        source, target = ((1, width_y + 1), (width_y, 0))[side]
        planes = pl.ds(1, width_x)
        return pltpu.make_async_remote_copy(
            src_ref=buf.at[planes, source], dst_ref=buf.at[planes, target],
            send_sem=y_send.at[which, side], recv_sem=y_recv.at[which, side],
            device_id={"gy": (gy - 1, gy + 1)[side]}, device_id_type=MESH,
        )

    there_x, there_y = (has_left, has_right), (has_down, has_up)

    def start_x(buf, which, c):
        for side in (0, 1):
            @pl.when(there_x[side])
            def _(side=side):
                x_copy(buf, which, c, side).start()

    def start_y(buf, which, side):
        @pl.when(there_y[side])
        def _():
            y_copy(buf, which, side).start()

    def arrive_x(buf, which, c):
        for side in (0, 1):
            @pl.when(there_x[1 - side])
            def _(side=side):
                x_copy(buf, which, c, side).wait_recv()

    def arrive_y(buf, which, side):
        @pl.when(there_y[1 - side])
        def _():
            y_copy(buf, which, side).wait_recv()

    start_y(v_ref, 0, 0)
    start_y(v_ref, 0, 1)
    for c in ROW_CHUNKS:
        start_x(v_ref, 0, c)
    tell(news_sem.at[0], rounds[0])

    z_lane = lax.broadcasted_iota(jnp.int32, (1, lanes), 1)

    def advance(src, x, y):
        def row(ref):
            return jnp.broadcast_to(ref, (k, lanes))

        i = x * width_y + y
        core = src[x + 1, y + 1]
        upper = jnp.where(z_lane < lanes - 1, nei_ref[4, pl.ds(i, 1), :], 0.0)
        lower = jnp.where(z_lane > 0, nei_ref[5, pl.ds(i, 1), :], 0.0)
        result = row(cen_ref[pl.ds(i, 1), :]) * core
        result = result + row(nei_ref[0, pl.ds(i, 1), :]) * src[x + 2, y + 1]
        result = result + row(nei_ref[1, pl.ds(i, 1), :]) * src[x, y + 1]
        result = result + row(nei_ref[2, pl.ds(i, 1), :]) * src[x + 1, y + 2]
        result = result + row(nei_ref[3, pl.ds(i, 1), :]) * src[x + 1, y]
        result = result + row(upper) * pltpu.roll(core, lanes - 1, 1)
        result = result + row(lower) * pltpu.roll(core, 1, 1)
        return result

    loads[3].wait()
    loads[4].wait()
    arrive_y(v_ref, 0, 0)
    arrive_y(v_ref, 0, 1)
    for c in ROW_CHUNKS:
        arrive_x(v_ref, 0, c)

        def first(i, _, c=c):
            x, y = i // 2, 2 * c + i % 2
            w_ref[x + 1, y + 1] = advance(v_ref, x, y)
            return 0

        lax.fori_loop(0, 2 * width_x, first, 0, unroll=True)
        start_x(w_ref, 1, c)
        if c == 0:
            start_y(w_ref, 1, 0)
        if c == width_y // 2 - 1:
            start_y(w_ref, 1, 1)
        if c == ROW_CHUNKS[0]:
            hear(0)
            tell(news_sem.at[1], rounds[1])
        if c == ROW_CHUNKS[-2]:
            hear(1)
            tell(news_sem.at[2], rounds[2])

    high = jnp.zeros((k, k), F32)
    low = jnp.zeros((k, k), F32)
    for c in ROW_CHUNKS:
        arrive_x(w_ref, 1, c)
        if c == 0:
            arrive_y(w_ref, 1, 1)
        if c == width_y // 2 - 1:
            arrive_y(w_ref, 1, 0)

        def second(i, most, c=c):
            x, y = i // 2, 2 * c + i % 2
            value = advance(w_ref, x, y)
            s_ref[c * 2 * width_x + i] = value
            return jnp.maximum(most, jnp.abs(value))

        most = lax.fori_loop(0, 2 * width_x, second, jnp.zeros((k, lanes), F32), unroll=True)
        big = power_below(jnp.max(most, axis=1, keepdims=True)) * F32(1.5 * 2**17)
        for i in range(2 * width_x):
            for j, piece in enumerate(pieces(s_ref[c * 2 * width_x + i], big)):
                xs_ref[c, j * k : (j + 1) * k, i * lanes : (i + 1) * lanes] = piece.astype(jnp.bfloat16)
        pltpu.make_async_copy(xs_ref.at[c], xs_out.at[c], store_sem.at[c]).start()
        part_high, part_low = outer_sums(xs_ref[c])
        high, e = two_sum(high, part_high)
        low = low + (part_low + e)

    pack_ref[...] = jnp.concatenate([high, low], axis=1)

    rows = k // ny
    y_rank = y_group.rank()

    def share(phase, group, source, target, slot, sem_slot):
        rank = group.rank()
        copies = []
        for step in far_first(group.size):
            peer = (rank + step) % group.size
            copies.append(pltpu.make_async_remote_copy(
                src_ref=source(peer), dst_ref=target(rank),
                send_sem=r_send.at[phase, step], recv_sem=r_recv.at[phase, rank],
                device_id={group.axis: group.member(peer)}, device_id_type=MESH,
            ))
        for copy in copies:
            copy.start()
        return copies

    def gather(phase, group, source, target):
        rank = group.rank()
        for step in range(1, group.size):
            peer = (rank + step) % group.size
            pltpu.make_async_remote_copy(
                src_ref=source(peer), dst_ref=target(peer),
                send_sem=r_send.at[phase, step], recv_sem=r_recv.at[phase, peer],
                device_id={group.axis: group.member(peer)}, device_id_type=MESH,
            ).wait_recv()

    sent = []

    def part_of(peer):
        return pack_ref.at[pl.ds(pl.multiple_of(peer * rows, rows), rows)]

    buf0[y_rank] = pack_ref[pl.ds(pl.multiple_of(y_rank * rows, rows), rows)]
    sent += share(0, y_group, part_of, lambda r: buf0.at[r], None, None)
    gather(0, y_group, part_of, lambda r: buf0.at[r])
    total = sum_slots(buf0, ny, lanes)
    for phase, (group, buf) in enumerate(zip(groups, (buf1, buf2)), 1):
        if phase == 2:
            hear(2)
        here = piece_ref.at[phase - 1]
        here[...] = total
        buf[group.rank()] = total
        sent += share(phase, group, lambda p: here, lambda r: buf.at[r], None, None)
        gather(phase, group, lambda p: here, lambda r: buf.at[r])
        total = sum_slots(buf, group.size, lanes)
    last = piece_ref.at[2]
    last[...] = total

    def rows_of(r):
        return g_out.at[pl.ds(pl.multiple_of(r * rows, rows), rows)]

    own_rows = pltpu.make_async_copy(last, rows_of(y_rank), own_sem)
    own_rows.start()
    sent += share(3, y_group, lambda p: last, rows_of, None, None)
    gather(3, y_group, lambda p: last, rows_of)
    own_rows.wait()

    for copy in sent:
        copy.wait_send()
    for c in ROW_CHUNKS:
        pltpu.make_async_copy(xs_ref.at[c], xs_out.at[c], store_sem.at[c]).wait()
        for which, buf in enumerate((v_ref, w_ref)):
            for side in (0, 1):
                @pl.when(there_x[side])
                def _(c=c, which=which, buf=buf, side=side):
                    x_copy(buf, which, c, side).wait_send()
    for which, buf in enumerate((v_ref, w_ref)):
        for side in (0, 1):
            @pl.when(there_y[side])
            def _(which=which, buf=buf, side=side):
                y_copy(buf, which, side).wait_send()


def eliminate(a):
    n, lanes = a.shape
    full = (8, lanes)
    blocks = [a[8 * i : 8 * i + 8] for i in range(n // 8)]
    sub = lax.broadcasted_iota(jnp.int32, full, 0)
    for p in range(n // 8):
        rest = range(p + 1, n // 8)
        own = blocks[p]

        def column(block, c, p=p):
            return jnp.broadcast_to(block[:, 8 * p + c : 8 * p + c + 1], full)

        rows = [jnp.broadcast_to(own[j : j + 1], full) for j in range(8)]
        own_columns = [column(own, c) for c in range(8)]
        d = {(i, c): jnp.broadcast_to(own_columns[c][i : i + 1], full) for c in range(8) for i in range(c + 1)}
        u = {i: [column(blocks[i], c) for c in range(8)] for i in rest}
        for j in range(8):
            scale = lax.rsqrt(d[j, j])
            rows[j] = rows[j] * scale
            factor = {c: d[j, c] * scale for c in range(j + 1, 8)}
            for c in range(j + 1, 8):
                for e in range(c, 8):
                    d[c, e] = d[c, e] - factor[c] * factor[e]
                rows[c] = rows[c] - factor[c] * rows[j]
            for i in rest:
                u[i][j] = u[i][j] * scale
                for c in range(j + 1, 8):
                    u[i][c] = u[i][c] - u[i][j] * factor[c]
                blocks[i] = blocks[i] - u[i][j] * rows[j]
        done = rows[0]
        for j in range(1, 8):
            done = jnp.where(sub == j, rows[j], done)
        blocks[p] = done
    return jnp.concatenate(blocks, axis=0)


def eye_mask(rows, columns):
    return lax.broadcasted_iota(jnp.int32, (rows, columns), 0) == lax.broadcasted_iota(jnp.int32, (rows, columns), 1)


def dot(a, b):
    return jnp.dot(a, b, precision=HIGHEST, preferred_element_type=F32)


def basis_kernel(root, xs_hbm, g_ref, modes_ref, r_hbm, first_hbm, xs_ref, out_ref, r_ref, first_ref, load_sem, store_sem, small_sem):
    k = g_ref.shape[0]
    load = pltpu.make_async_copy(xs_hbm, xs_ref, load_sem)
    load.start()
    high, low = g_ref[:, :k], g_ref[:, k:]
    eye = eye_mask(k, k).astype(F32)
    row, column = lax.broadcasted_iota(jnp.int32, (k, k), 0), lax.broadcasted_iota(jnp.int32, (k, k), 1)
    upper = row <= column

    done = eliminate(jnp.concatenate([high, eye], axis=1))
    first = jnp.where(upper, done[:, :k], 0.0).T
    inverse = done[:, k:]
    parts = cut(first)
    first = (parts[2].astype(F32) + parts[1].astype(F32)) + parts[0].astype(F32)
    full, rest = outer_sums(jnp.concatenate(parts, axis=0))
    left = (high - full) + (low - rest)
    gram = eye + dot(dot(inverse, left), inverse.T)

    done = eliminate(jnp.concatenate([gram, eye], axis=1))
    second_t = jnp.where(upper, done[:, :k], 0.0)
    weights = jnp.concatenate([jnp.concatenate([p] * 3, axis=1) for p in cut(dot(done[:, k:], inverse) * root)], axis=0)
    load.wait()
    chunks, lanes = xs_ref.shape[0], out_ref.shape[-1]
    width_x, _, width_y, _ = out_ref.shape
    flat = out_ref.reshape(width_x, k * width_y, lanes)
    stores = []
    for x in range(width_x):
        for c in range(chunks):
            prod = jnp.dot(weights, xs_ref[c, :, 2 * lanes * x : 2 * lanes * (x + 1)], preferred_element_type=F32)
            prod = prod[:k] + (prod[k : 2 * k] + prod[2 * k :])
            for i in range(2):
                flat[x, pl.ds(2 * c + i, k, stride=width_y), :] = prod[:, i * lanes : (i + 1) * lanes]
        stores.append(pltpu.make_async_copy(out_ref.at[x], modes_ref.at[:, x], store_sem.at[x]))
        stores[-1].start()
    small = [
        pltpu.make_async_copy(source, target, small_sem.at[i])
        for i, (source, target) in enumerate(((first_ref, first_hbm), (r_ref, r_hbm)))
    ]
    first_ref[...] = first.T * (1.0 / root)
    small[0].start()
    r_ref[...] = dot(second_t, first.T) * (1.0 / root)
    small[1].start()
    for store in stores + small:
        store.wait()


def local(nx, ny, background, sensor_cells, sensor_gain, center, neighbours):
    k, width_x, width_y, lanes = background.shape
    cells = width_x * width_y
    groups = groups_of(nx)
    vmem = pl.BlockSpec(memory_space=pltpu.VMEM)
    dma = pltpu.SemaphoreType.DMA
    slots = max([ny] + [g.size for g in groups])
    rows = k // ny
    pieces_shape = (width_y // 2, 3 * k, 2 * width_x * lanes)
    fields, gram = pl.pallas_call(
        functools.partial(fields_kernel, nx, ny),
        out_shape=(jax.ShapeDtypeStruct(pieces_shape, jnp.bfloat16), jax.ShapeDtypeStruct((k, 2 * k), F32)),
        in_specs=[pl.BlockSpec(memory_space=pltpu.HBM)] * 5,
        out_specs=(pl.BlockSpec(memory_space=pltpu.HBM), pl.BlockSpec(memory_space=pltpu.HBM)),
        scratch_shapes=[
            pltpu.SMEM((k,), jnp.int32),
            pltpu.SMEM((k,), F32),
            pltpu.VMEM((cells, lanes), F32),
            pltpu.VMEM((6, cells, lanes), F32),
            pltpu.VMEM((k * cells, lanes), F32),
            pltpu.VMEM((width_x + 2, width_y + 2, k, lanes), F32),
            pltpu.VMEM((width_x + 2, width_y + 2, k, lanes), F32),
            pltpu.VMEM((cells, k, lanes), F32),
            pltpu.VMEM((k, lanes), jnp.int32),
            pltpu.VMEM((k, lanes), F32),
            pltpu.VMEM(pieces_shape, jnp.bfloat16),
            pltpu.VMEM((k, 2 * k), F32),
            pltpu.VMEM((3, rows, 2 * k), F32),
            pltpu.VMEM((ny, rows, 2 * k), F32),
            pltpu.VMEM((groups[0].size, rows, 2 * k), F32),
            pltpu.VMEM((groups[1].size, rows, 2 * k), F32),
            pltpu.SemaphoreType.REGULAR((3,)), dma, dma((5,)), dma((4,)),
            dma((2, 2, 4)), dma((2, 2, 4)), dma((2, 2)), dma((2, 2)),
            dma((4, slots)), dma((4, slots)),
        ],
        compiler_params=pltpu.CompilerParams(
            collective_id=0, has_side_effects=True, vmem_limit_bytes=56 * 2**20
        ),
        name="fields_and_products",
    )(
        sensor_cells, sensor_gain, background.reshape(k * cells, lanes),
        center.reshape(cells, lanes), neighbours.reshape(6, cells, lanes),
    )
    total_cells = cells * lanes * nx * ny
    root = float(total_cells) ** 0.5
    modes, r_factor, first_r = pl.pallas_call(
        functools.partial(basis_kernel, root),
        out_shape=(
            jax.ShapeDtypeStruct(background.shape, F32),
            jax.ShapeDtypeStruct((k, k), F32),
            jax.ShapeDtypeStruct((k, k), F32),
        ),
        in_specs=[pl.BlockSpec(memory_space=pltpu.HBM), vmem],
        out_specs=(pl.BlockSpec(memory_space=pltpu.HBM),) * 3,
        scratch_shapes=[
            pltpu.VMEM(pieces_shape, jnp.bfloat16), pltpu.VMEM((width_x, k, width_y, lanes), F32),
            pltpu.VMEM((k, k), F32), pltpu.VMEM((k, k), F32), dma, dma((width_x,)), dma((2,)),
        ],
        compiler_params=pltpu.CompilerParams(vmem_limit_bytes=56 * 2**20),
        name="basis",
    )(fields, gram)
    return modes, r_factor, first_r


def solution(mesh):
    nx, ny = mesh.shape["gx"], mesh.shape["gy"]
    in_specs = (P(None, "gx", "gy", None), P(), P(), P("gx", "gy", None), P(None, "gx", "gy", None))
    out_specs = (P(None, "gx", "gy", None), P(), P())
    return jax.shard_map(
        functools.partial(local, nx, ny), mesh=mesh, in_specs=in_specs, out_specs=out_specs, check_vma=False
    )
```
